128 devices in a mesh: gx: 8 (over z, core), gy: 16 (over y, x).
Axes of the slice: x: 4, y: 4, z: 4, core: 2. Of those that a mesh axis runs over, the one named last changes fastest.
Arguments:
- irreps: bfloat16 [8, 16, 128, 25, 128], P('gx', 'gy'), may hold values from -6 to 6
- mix_weight: bfloat16 [5, 128, 128], replicated, may hold values from -0.5 to 0.5
- readout: bfloat16 [25, 128], replicated, may hold values from -0.5 to 0.5
- ghost_x: int32 [8, 16, 2, 64], P('gx', 'gy'), may hold values from 0 to 127
- ghost_y: int32 [8, 16, 2, 64], P('gx', 'gy'), may hold values from 0 to 255
- edge_source_row: int32 [8, 16, 2048], P('gx', 'gy'), may hold values from 0 to 383
- edge_dst: int32 [8, 16, 2048], P('gx', 'gy'), may hold values from 0 to 128
- radial: float32 [8, 16, 25, 2048], P('gx', 'gy'), may hold values from -4 to 4
- tile_peer: int32 [8, 16, 32, 4], P('gx', 'gy'), may hold values from 0 to 127, all different within a row; in each aligned block of 32 rows (0 to 31, 32 to 63, ..., all dimensions but the last counted through in order) at most 2 rows name the same one
- tile_block: int32 [8, 16, 32, 4], P('gx', 'gy'), may hold values from 0 to 15
- tile_count: int32 [8, 16, 32], P('gx', 'gy'), may hold values from 1 to 4
- basis: bfloat16 [8, 16, 32, 200, 256], P('gx', 'gy'), may hold values from -0.21875 to 0.21875
- density_cot: bfloat16 [8, 16, 2048], P('gx', 'gy'), may hold values from -6 to 6
Outputs:
- density: float32 [8, 16, 2048], P('gx', 'gy')
- grad_weights: float32 [5, 128, 128], replicated
The draws below stay inside these ranges and needn't reach their ends.
Inputs may be any that keep to these rules, and one draw needn't show every extreme that they name: `tile_peer`: among the 32 x 4 slots of one pencil, used or not, no brick is named more than 2 times, a bound that some block reaches; the slots of one tile name different bricks. `edge_dst`: an edge slot whose destination is 128 is padding.
All inputs are finite; a program needn't handle non-finite values.
Results may differ from the reference program's by a relative error of at most 0.014.
Values may be sent and summed in bfloat16 or wider, within the bound.
A program may use at most 192 MiB of HBM per device.

```python
import math
import jax
import jax.numpy as jnp
import numpy as np
from jax import lax

ATOMS_DEV = 128
CHAN = 128
LMAX = 4
COMPS = 25
EDGES_DEV = 2048
GHOSTS = 64
BLK = 8
NBLK = 16
TILES_DEV = 32
PTS = 64
K = 4
CAP = 2
N_GX = 8
N_GY = 16
DEVICES = 128


def set_ends(drawn, key, smallest, top_value):
    spot = [jax.random.randint(jax.random.fold_in(key, axis), (), 0, length) for axis, length in enumerate(drawn.shape)]
    widest = drawn.shape.index(max(drawn.shape))
    neighbour = spot[:widest] + [(spot[widest] + 1) % drawn.shape[widest]] + spot[widest + 1:]
    return drawn.at[tuple(spot)].set(smallest).at[tuple(neighbour)].set(top_value)


def steps_of(stream_key, shape, cuts, least, high):
    gain, own = 1.0, jax.random.fold_in(stream_key, 6)
    for position, shards_of in cuts:
        heights = jnp.exp(jax.random.uniform(jax.random.fold_in(own, position), (shards_of,), jnp.float32, least / len(cuts), high / len(cuts)))
        gain = gain * jnp.repeat(heights, shape[position] // shards_of).reshape([-1 if axis == position else 1 for axis in range(len(shape))])
    return gain


def deal_out(stream_key, own, number, rows, count, top, most, lean):
    order = jax.random.permutation(stream_key, count)
    crowded, ordinary = portions_of(count, rows * top, most, lean, True), portions_of(count, rows * top, most, lean, False)
    places = jnp.arange(count)

    def named(lengths, rotation):
        used = int((lengths > 0).sum())
        fixed = max(1, used // 4)
        passed = fixed + (places - fixed + rotation * (used - fixed)) % max(1, count - fixed)
        return jnp.zeros((count,), jnp.int32).at[order[jnp.where(places < fixed, places, passed)]].set(jnp.asarray(lengths, jnp.int32))

    lengths = jnp.where(number % 4 == 0, named(crowded, number // 4), named(ordinary, number - number // 4 - 1))
    mixed = jax.random.permutation(jax.random.fold_in(own, 3), count)
    giver, sink = mixed[0:count // 2 * 2:2], mixed[1:count // 2 * 2:2]
    margin = jnp.minimum(lengths[giver] - 1, most - lengths[sink]) // 2
    margin = jnp.where((giver == order[0]) | (sink == order[0]) | (lengths[sink] == 0), 0, jnp.maximum(margin, 0))
    passed = jax.random.randint(jax.random.fold_in(own, 4), (count // 2,), 0, 1 << 20) % (margin + 1)
    lengths = lengths.at[giver].add(-passed).at[sink].add(passed)
    members = jnp.searchsorted(jnp.cumsum(lengths), jnp.arange(rows * top), side="right").astype(jnp.int32)
    listing = members.reshape(top, rows).T
    listing = listing[jax.random.permutation(jax.random.fold_in(own, 1), rows)]
    rotation = jax.random.randint(jax.random.fold_in(own, 2), (rows, 1), 0, top)
    return jnp.take_along_axis(listing, (jnp.arange(top)[None, :] + rotation) % top, axis=1)


def portions_of(amount, total, most, lean, full):
    portions = [(1 << 20) // math.isqrt(standing ** lean) + 1 for standing in range(1, amount + 1)]
    largest = most if full else min(most, max(-(-total // amount), total * portions[0] // sum(portions)))
    least = 1 if total - largest >= amount - 1 else 0
    holding, spare = [largest] + [least] * (amount - 1), total - largest - least * (amount - 1)
    while spare > 0:
        candidates = [i for i in range(1, amount) if holding[i] < largest] or [i for i in range(1, amount) if holding[i] < most]
        pool, left = sum([portions[i] for i in candidates]), spare
        for i in candidates:
            extra = min(most - holding[i], max(1, left * portions[i] // pool), spare)
            holding[i] = holding[i] + extra
            spare = spare - extra
    return np.array(holding)


def scatter_about(key, dims, width, reach, shards=(), dtype=jnp.bfloat16):
    level = steps_of(key, dims, shards, -0.22, 0.18) if shards else 1.0
    drawn = jax.random.normal(key, dims, jnp.float32) * width * level
    return jnp.minimum(jnp.maximum(drawn, -reach), reach).astype(dtype)


def setup_inputs(seed: int = 0) -> dict:
    key_list = jax.random.split(jax.random.key(seed), 14)
    irreps = scatter_about(key_list[0], (N_GX, N_GY, ATOMS_DEV, COMPS, CHAN), 1.0, 6.0, ((0, 8), (1, 16)))
    mix_weight = scatter_about(key_list[1], (LMAX + 1, CHAN, CHAN), CHAN ** -0.5, 0.5)
    readout = scatter_about(key_list[2], (COMPS, CHAN), CHAN ** -0.5, 0.5)
    ghost_x = set_ends(jax.random.randint(key_list[3], (N_GX, N_GY, 2, GHOSTS), 0, ATOMS_DEV), jax.random.fold_in(key_list[3], 1), 0, ATOMS_DEV - 1).astype(jnp.int32)
    ghost_y = set_ends(jax.random.randint(key_list[4], (N_GX, N_GY, 2, GHOSTS), 0, ATOMS_DEV + 2 * GHOSTS), jax.random.fold_in(key_list[4], 1), 0, (ATOMS_DEV + 2 * GHOSTS) - 1).astype(jnp.int32)
    edge_source_row = set_ends(jax.random.randint(key_list[5], (N_GX, N_GY, EDGES_DEV), 0, ATOMS_DEV + 4 * GHOSTS), jax.random.fold_in(key_list[5], 1), 0, (ATOMS_DEV + 4 * GHOSTS) - 1).astype(jnp.int32)
    edge_dst = set_ends(jax.random.randint(key_list[6], (N_GX, N_GY, EDGES_DEV), 0, ATOMS_DEV + 1), jax.random.fold_in(key_list[6], 1), 0, ATOMS_DEV).astype(jnp.int32)
    radial = scatter_about(key_list[7], (N_GX, N_GY, COMPS, EDGES_DEV), 0.5, 4.0, ((0, 8), (1, 16)), jnp.float32)
    tile_peer_keys = jax.random.split(jax.random.fold_in(key_list[8], 1), N_GX * N_GY * TILES_DEV // TILES_DEV)
    tile_peer_turns = jax.random.permutation(jax.random.fold_in(key_list[8], 3), N_GX * N_GY * TILES_DEV // TILES_DEV)
    tile_peer = jax.vmap(lambda own, number: deal_out(jax.random.fold_in(key_list[8], 2), own, number, TILES_DEV, DEVICES, K, CAP, 2))(tile_peer_keys, tile_peer_turns).reshape((N_GX, N_GY, TILES_DEV, K))
    tile_block = set_ends(jax.random.randint(key_list[9], (N_GX, N_GY, TILES_DEV, K), 0, NBLK), jax.random.fold_in(key_list[9], 1), 0, NBLK - 1).astype(jnp.int32)
    tile_count = set_ends(jax.random.randint(key_list[10], (N_GX, N_GY, TILES_DEV), 1, K + 1), jax.random.fold_in(key_list[10], 1), 1, K).astype(jnp.int32)
    basis = scatter_about(key_list[11], (N_GX, N_GY, TILES_DEV, BLK * COMPS, K * PTS), (K * BLK * COMPS) ** -0.5, 0.21875, ((0, 8), (1, 16)))
    density_cot = scatter_about(key_list[12], (N_GX, N_GY, TILES_DEV * PTS), 1.0, 6.0, ((0, 8), (1, 16)))
    return {"irreps": irreps, "mix_weight": mix_weight, "readout": readout, "ghost_x": ghost_x, "ghost_y": ghost_y, "edge_source_row": edge_source_row, "edge_dst": edge_dst, "radial": radial, "tile_peer": tile_peer, "tile_block": tile_block, "tile_count": tile_count, "basis": basis, "density_cot": density_cot}


def degree_mix(feature, weights):
    pieces = []
    for degree in range(LMAX + 1):
        lower = degree * degree
        upper = (degree + 1) * (degree + 1)
        pieces.append(jnp.einsum("...lc,ce->...le", feature[..., lower:upper, :].astype(jnp.float32), weights[degree].astype(jnp.float32)))
    return jnp.concatenate(pieces, axis=-2)


def take_rows(source, indices):
    return jax.vmap(lambda rows_here, index_here: rows_here[index_here])(source, indices)


def add_rows(target, indices, values):
    return jax.vmap(lambda rows_here, index_here, value_here: rows_here.at[index_here].add(value_here))(target, indices, values)


def to_flat(array):
    return array.reshape((N_GX * N_GY,) + array.shape[2:])


def to_grid(array):
    return array.reshape((N_GX, N_GY) + array.shape[1:])


def reference(irreps, mix_weight, readout, ghost_x, ghost_y, edge_source_row, edge_dst, radial, tile_peer, tile_block, tile_count, basis, density_cot):
    processor_list = N_GX * N_GY
    mixed_rows = degree_mix(irreps, mix_weight).astype(jnp.bfloat16)
    face_x = to_grid(take_rows(to_flat(mixed_rows), to_flat(ghost_x)))
    from_left = jnp.roll(face_x[:, :, 1], 1, axis=0)
    from_right = jnp.roll(face_x[:, :, 0], -1, axis=0)
    first_table = jnp.concatenate([mixed_rows, from_left, from_right], axis=2)
    face_y = to_grid(take_rows(to_flat(first_table), to_flat(ghost_y)))
    from_lower = jnp.roll(face_y[:, :, 1], 1, axis=1)
    from_upper = jnp.roll(face_y[:, :, 0], -1, axis=1)
    full_table = jnp.concatenate([first_table, from_lower, from_upper], axis=2)
    readout_f = readout.astype(jnp.float32)

    def forward_device(inputs):
        table_rows, feature, sources, targets, edge_weight_table = inputs
        message = jnp.transpose(edge_weight_table)[:, :, None] * table_rows[sources].astype(jnp.float32)
        gathered = jax.ops.segment_sum(message, targets, num_segments=ATOMS_DEV + 1)[:ATOMS_DEV]
        gating = jax.nn.sigmoid(gathered[:, 0, :])
        updated = (feature.astype(jnp.float32) + gating[:, None, :] * gathered).astype(jnp.bfloat16)
        coefficient = jnp.sum(updated.astype(jnp.float32) * readout_f, axis=-1)
        return gathered, coefficient.reshape(NBLK, BLK * COMPS).astype(jnp.bfloat16)

    gathered_all, coefficient_all = lax.map(forward_device, (to_flat(full_table), to_flat(irreps), to_flat(edge_source_row), to_flat(edge_dst), to_flat(radial)))
    peer_ids = to_flat(tile_peer)
    wanted = to_flat(tile_block)
    is_live = (jnp.arange(K)[None, None, :] < to_flat(tile_count)[:, :, None]).astype(jnp.float32)
    fetched = coefficient_all[peer_ids, wanted]
    masked = fetched.astype(jnp.float32) * is_live[..., None]
    basis_f = to_flat(basis).astype(jnp.float32).reshape(processor_list, TILES_DEV, BLK * COMPS, K, PTS)
    density = jnp.einsum("dtjkp,dtkj->dtp", basis_f, masked)
    density = to_grid(density.reshape(processor_list, TILES_DEV * PTS))
    cotangent = to_flat(density_cot).astype(jnp.float32).reshape(processor_list, TILES_DEV, PTS)
    slot_grad = jnp.einsum("dtjkp,dtp->dtkj", basis_f, cotangent) * is_live[..., None]
    block_grad = jnp.zeros((processor_list, NBLK, BLK * COMPS), jnp.float32).at[peer_ids, wanted].add(slot_grad)

    def backward_per_processor(inputs):
        grad_blocks, gathered, sources, targets, edge_weight_table = inputs
        atom_grad = grad_blocks.reshape(ATOMS_DEV, COMPS)
        grad_updated = atom_grad[:, :, None] * readout_f
        gating = jax.nn.sigmoid(gathered[:, 0, :])
        grad_gathered = grad_updated * gating[:, None, :]
        grad_gate = jnp.sum(grad_updated * gathered, axis=1) * gating * (1.0 - gating)
        grad_gathered = grad_gathered.at[:, 0, :].add(grad_gate)
        padded_grad = jnp.concatenate([grad_gathered, jnp.zeros((1, COMPS, CHAN), jnp.float32)], axis=0)
        grad_message = jnp.transpose(edge_weight_table)[:, :, None] * padded_grad[targets]
        return jax.ops.segment_sum(grad_message, sources, num_segments=ATOMS_DEV + 4 * GHOSTS)

    grad_table = to_grid(lax.map(backward_per_processor, (block_grad, gathered_all, to_flat(edge_source_row), to_flat(edge_dst), to_flat(radial))))
    tail_start = ATOMS_DEV + 2 * GHOSTS
    grad_first = grad_table[:, :, :tail_start]
    grad_first = to_grid(add_rows(to_flat(grad_first), to_flat(ghost_y[:, :, 1]), to_flat(jnp.roll(grad_table[:, :, tail_start:tail_start + GHOSTS], -1, axis=1))))
    grad_first = to_grid(add_rows(to_flat(grad_first), to_flat(ghost_y[:, :, 0]), to_flat(jnp.roll(grad_table[:, :, tail_start + GHOSTS:], 1, axis=1))))
    grad_mixed = grad_first[:, :, :ATOMS_DEV]
    grad_mixed = to_grid(add_rows(to_flat(grad_mixed), to_flat(ghost_x[:, :, 1]), to_flat(jnp.roll(grad_first[:, :, ATOMS_DEV:ATOMS_DEV + GHOSTS], -1, axis=0))))
    grad_mixed = to_grid(add_rows(to_flat(grad_mixed), to_flat(ghost_x[:, :, 0]), to_flat(jnp.roll(grad_first[:, :, ATOMS_DEV + GHOSTS:tail_start], 1, axis=0))))
    grad_low = grad_mixed.astype(jnp.bfloat16)
    results = []
    for degree in range(LMAX + 1):
        lower = degree * degree
        upper = (degree + 1) * (degree + 1)
        results.append(jnp.einsum("xyalc,xyale->ce", irreps[:, :, :, lower:upper, :].astype(jnp.float32), grad_low[:, :, :, lower:upper, :].astype(jnp.float32)))
    return density, jnp.stack(results)
```

```python
import functools

import jax
import jax.numpy as jnp
from jax import lax
from jax.experimental import pallas as pl
from jax.experimental.pallas import tpu as pltpu
from jax.sharding import PartitionSpec as P

MESH = pl.DeviceIdType.MESH
BF = jnp.bfloat16
F32 = jnp.float32

CHUNKS = ((0, 4), (16, 21), (21, 25), (9, 13), (13, 16), (4, 9))
DEGREES = 5


def degree_of(m):
    l = 0
    while (l + 1) * (l + 1) <= m:
        l += 1
    return l


def iota(shape, dim):
    return lax.broadcasted_iota(jnp.int32, shape, dim)


def dot(a, b):
    return jnp.dot(a, b, preferred_element_type=F32)


def dot_nt(a, b):
    return lax.dot_general(a, b, (((1,), (1,)), ((), ())), preferred_element_type=F32)


def dot_tn(a, b):
    return lax.dot_general(a, b, (((0,), (0,)), ((), ())), preferred_element_type=F32)


def kernel(
    nx, ny,
    irr, w, ro, small, src, dst, rad, cot, basis_hbm,
    dens_out, gw_out,
    basis, ghost, xface, yface, hot_x, hot_y, source_hot, dst_mask, scaled, op,
    y_st, g_st, gg_st, gate, coef, gate_grad, atom_grad, tmp256,
    s_a, r_a, s_b, r_b, s_c, r_c, s_d, r_d, pick_p, own_hot, dens,
    gw_send, gw_recv, sum_x_send, sum_x, sum_y, out_recv,
    basis_sem, xs_sem, xr_sem, ys_sem, yr_sem,
    as_sem, ar_sem, bs_sem, br_sem, cs_sem, cr_sem, ds_sem, dr_sem,
    ws_sem, wr_sem, us_sem, ur_sem, vs_sem, vr_sem, os_sem, or_sem,
):
    ix = lax.axis_index("gx")
    iy = lax.axis_index("gy")
    yq, yr = iy // 4, iy % 4
    left, right = (ix + nx - 1) % nx, (ix + 1) % nx
    lower, upper = (iy + ny - 1) % ny, (iy + 1) % ny

    basis_copy = pltpu.make_async_copy(basis_hbm, basis, basis_sem)
    basis_copy.start()

    barrier = pltpu.get_barrier_semaphore()

    def greet_x(d, c):
        pl.semaphore_signal(barrier, inc=1, device_id=((ix + d) % nx, iy), device_id_type=MESH)
        return c

    def greet_y(d, c):
        pl.semaphore_signal(barrier, inc=1, device_id=(ix, (iy + d) % ny), device_id_type=MESH)
        return c

    lax.fori_loop(1, nx, greet_x, 0)
    lax.fori_loop(1, ny, greet_y, 0)

    def remote(s, d, ssem, rsem, i, j):
        return pltpu.make_async_remote_copy(
            src_ref=s, dst_ref=d, send_sem=ssem, recv_sem=rsem, device_id=(i, j), device_id_type=MESH
        )

    def x_copies(c):
        lo, hi = CHUNKS[c]
        n = hi - lo
        return (
            remote(xface.at[pl.ds(lo, n), pl.ds(64, 64), :], ghost.at[pl.ds(lo, n), pl.ds(0, 64), :],
                   xs_sem.at[c, 0], xr_sem.at[c, 0], right, iy),
            remote(xface.at[pl.ds(lo, n), pl.ds(0, 64), :], ghost.at[pl.ds(lo, n), pl.ds(64, 64), :],
                   xs_sem.at[c, 1], xr_sem.at[c, 1], left, iy),
        )

    def y_copies(c):
        lo, hi = CHUNKS[c]
        n = hi - lo
        return (
            remote(yface.at[pl.ds(lo, n), pl.ds(64, 64), :], ghost.at[pl.ds(lo, n), pl.ds(128, 64), :],
                   ys_sem.at[c, 0], yr_sem.at[c, 0], ix, upper),
            remote(yface.at[pl.ds(lo, n), pl.ds(0, 64), :], ghost.at[pl.ds(lo, n), pl.ds(192, 64), :],
                   ys_sem.at[c, 1], yr_sem.at[c, 1], ix, lower),
        )

    sm = small[...]
    hot_x[...] = jnp.where(iota((128, 128), 0) == sm[0:1, :], 1.0, 0.0).T.astype(BF)

    def send_x(c):
        lo, hi = CHUNKS[c]
        chooser = hot_x[...]
        for m in range(lo, hi):
            xface[m] = dot(chooser, irr[m]).astype(BF)
        if c == 0:
            pl.semaphore_wait(barrier, nx + ny - 2)
        for copy in x_copies(c):
            copy.start()

    for c in range(len(CHUNKS)):
        send_x(c)

    for half in range(2):
        hot_y[:, half * 128:(half + 1) * 128] = (
            jnp.where(iota((128, 128), 0) + half * 128 == sm[1:2, :], 1.0, 0.0).T.astype(BF)
        )

    def send_y(c):
        for copy in x_copies(c):
            copy.wait_recv()
        lo, hi = CHUNKS[c]
        for m in range(lo, hi):
            rows = dot(hot_y[:, 0:128], irr[m]) + dot(hot_y[:, 128:256], ghost[m, 0:128, :])
            yface[m] = rows.astype(BF)
        for copy in y_copies(c):
            copy.start()

    src_cols = jnp.concatenate([src[...].astype(F32), jnp.zeros((112, 128), F32)], axis=0).T
    lane384 = iota((128, 384), 1).astype(F32)
    sub128 = iota((128, 128), 0)
    for k in range(16):
        source_hot[k * 128:(k + 1) * 128, :] = jnp.where(src_cols[:, k:k + 1] == lane384, 1.0, 0.0).astype(BF)
        dst_mask[:, k * 128:(k + 1) * 128] = jnp.where(sub128 == dst[k:k + 1, :], 1.0, 0.0).astype(BF)

    def build_op(c):
        lo, hi = CHUNKS[c]
        n = hi - lo
        for i in range(n):
            row = rad[lo + i].astype(BF)
            scaled[i * 128:(i + 1) * 128, :] = dst_mask[...] * jnp.broadcast_to(row, (128, 2048))
        built = dot(scaled[0:n * 128, :], source_hot[...])
        for i in range(n):
            op[lo + i] = built[i * 128:(i + 1) * 128, :].astype(BF)

    send_y(0)
    build_op(0)

    peer_row = sm[2:3, :]
    same = (jnp.broadcast_to(peer_row, (128, 128)).astype(F32).T == peer_row.astype(F32)) & (
        iota((128, 128), 0) < iota((128, 128), 1)
    )
    rank = jnp.sum(jnp.where(same, 1.0, 0.0), axis=0, keepdims=True).astype(jnp.int32)
    live_row = (iota((1, 128), 1) % 4) < sm[4:5, :]
    position = jnp.where(live_row, peer_row * 2 + rank, -1)
    chosen = jnp.where(iota((256, 128), 0) == position, 1.0, 0.0)
    for half in range(2):
        pick_p[:, half * 128:(half + 1) * 128] = chosen[half * 128:(half + 1) * 128, :].T.astype(BF)
    spread = jnp.where(iota((128, 16), 1) == iota((128, 16), 0) // 8, 1.0, 0.0).astype(BF)
    picked = dot(spread, cot[...])
    rolled = pltpu.roll(picked, 64, 1)
    odd = (iota((128, 128), 0) // 4) % 2
    mine = jnp.where((iota((128, 128), 1) // 64) == odd, picked, rolled)
    both = jnp.concatenate([mine, mine], axis=1)
    weights = jnp.where(iota((128, 256), 1) // 64 == iota((128, 256), 0) % 4, both, 0.0).astype(BF)

    send_y(1)
    basis_copy.wait()

    lane_tile = iota((200, 128), 1) // 4

    def slot_step(t, acc):
        return jnp.where(lane_tile == t, dot_nt(basis[t], weights), acc)

    slot_grad = lax.fori_loop(0, 32, slot_step, jnp.zeros((200, 128), F32))
    id_rows = jnp.where(iota((56, 128), 0) == 0, jnp.broadcast_to(sm[3:4, :].astype(F32), (56, 128)), 0.0)
    tmp256[...] = jnp.concatenate([slot_grad, id_rows], axis=0)
    sent = dot_nt(chosen.astype(BF), tmp256[...].astype(BF)).astype(BF)
    for k in range(nx):
        s_a[k] = sent[k * 32:(k + 1) * 32, :]
    r_a[ix] = s_a[ix]

    def exchange(axis, n, s, r, ssem, rsem, start):
        me = ix if axis == "x" else iy

        def step(d, c):
            other = (me + d) % n
            to = (other, iy) if axis == "x" else (ix, other)
            if start == "recv":
                remote(s.at[other], r.at[other], ssem.at[other], rsem.at[other], *to).wait_recv()
                return c
            copy = remote(s.at[other], r.at[me], ssem.at[other], rsem.at[me], *to)
            if start == "start":
                copy.start()
            else:
                copy.wait_send()
            return c

        lax.fori_loop(1, n, step, 0)

    exch_a = functools.partial(exchange, "x", nx, s_a, r_a, as_sem, ar_sem)
    exch_b = functools.partial(exchange, "y", ny, s_b, r_b, bs_sem, br_sem)
    exch_c = functools.partial(exchange, "y", ny, s_c, r_c, cs_sem, cr_sem)
    exch_d = functools.partial(exchange, "x", nx, s_d, r_d, ds_sem, dr_sem)
    exch_a("start")

    send_y(2)
    send_y(3)
    send_y(4)
    send_y(5)
    build_op(1)

    n_i, n_j = iota((256, 256), 0), iota((256, 256), 1)
    turned = (n_i % 16) // 2 * 32 + n_i // 16 * 2 + n_i % 2
    turn = jnp.where(n_j == turned, 1.0, 0.0).astype(BF)
    back = jnp.where(n_j == n_i % 32 // 2 * 16 + n_i // 32 * 2 + n_i % 2, 1.0, 0.0).astype(BF)
    exch_a("recv")
    rows = dot(turn, r_a[...].reshape(256, 256)).astype(BF)
    for k in range(ny):
        s_b[k] = rows[k * 16:(k + 1) * 16, :]
    r_b[iy] = s_b[iy]
    exch_b("start")

    build_op(2)
    build_op(3)

    ro_f = ro[...].astype(F32)
    ro_cols = jnp.concatenate([ro_f, jnp.zeros((103, 128), F32)], axis=0).T
    lane128 = iota((128, 128), 1)
    coef[...] = jnp.zeros((128, 128), F32)

    def forward(c):
        for copy in y_copies(c):
            copy.wait_recv()
        lo, hi = CHUNKS[c]
        total = coef[...]
        for m in range(lo, hi):
            y = dot(op[m, :, 0:128], irr[m]) + dot(op[m, :, 128:384], ghost[m])
            y = y.astype(BF)
            y_st[m] = y
            g = dot(y, w[degree_of(m)])
            g_st[m] = g
            if m == 0:
                gate[...] = jax.nn.sigmoid(g)
            updated = (irr[m].astype(F32) + gate[...] * g).astype(BF)
            total = total + dot(updated, jnp.where(lane128 == m, ro_cols, 0.0).astype(BF))
        coef[...] = total

    def backward(c):
        lo, hi = CHUNKS[c]
        total = gate_grad[...]
        ag = atom_grad[...]
        for m in range(lo, hi):
            gu = ag[:, m:m + 1] * ro_f[m:m + 1, :]
            total = total + gu * g_st[m]
            if m > 0:
                gg_st[m] = (gu * gate[...]).astype(BF)
        gate_grad[...] = total

    def weight_grad(l):
        lo, hi = l * l, (l + 1) * (l + 1)
        n = (hi - lo) * 128
        part = dot_tn(y_st[lo:hi].reshape(n, 128), gg_st[lo:hi].reshape(n, 128)).astype(BF)
        for k in range(nx):
            gw_send[l, k] = part[k * 16:(k + 1) * 16, :]
        gw_recv[l, ix] = gw_send[l, ix]
        exchange("x", nx, gw_send.at[l], gw_recv.at[l], ws_sem.at[l], wr_sem.at[l], "start")

    forward(0)
    build_op(4)
    build_op(5)
    forward(1)

    exch_b("recv")
    incoming = r_b[...].reshape(256, 256)
    ids = incoming[:, 128:256].astype(F32)[:, 72:73]
    owner = jnp.where(ids == iota((256, 128), 1).astype(F32), 1.0, 0.0)
    own_hot[...] = owner.astype(BF)
    owner_t = jnp.concatenate([owner[0:128, :].T[0:16, :], owner[128:256, :].T[0:16, :]], axis=1).astype(BF)
    block_grad = dot(owner_t, incoming)
    for j in range(8):
        moved = block_grad if j == 0 else pltpu.roll(block_grad, 256 - 25 * j, 1)
        atom_grad[pl.ds(j, 16, stride=8), :] = moved[:, 0:128]
    gate_grad[...] = jnp.zeros((128, 128), F32)

    backward(0)
    backward(1)
    weight_grad(1)
    forward(2)
    backward(2)
    weight_grad(4)
    forward(3)
    backward(3)
    forward(4)
    backward(4)
    weight_grad(3)
    forward(5)

    coef_rows = jnp.zeros((16, 256), F32)
    valid = jnp.where(iota((16, 256), 1) < 25, 1.0, 0.0)
    for j in range(8):
        part = jnp.concatenate([coef[pl.ds(j, 16, stride=8), :], jnp.zeros((16, 128), F32)], axis=1) * valid
        coef_rows = coef_rows + (part if j == 0 else pltpu.roll(part, 25 * j, 1))
    coef_pad = jnp.concatenate([coef_rows, jnp.zeros((112, 256), F32)], axis=0).astype(BF)
    answer = dot(own_hot[...], coef_pad).astype(BF)
    for k in range(ny):
        s_c[k] = answer[k * 16:(k + 1) * 16, :]
    r_c[iy] = s_c[iy]
    exch_c("start")

    backward(5)
    weight_grad(2)
    gu = atom_grad[:, 0:1] * ro_f[0:1, :]
    s = gate[...]
    gg_st[0] = (gu * s + gate_grad[...] * s * (1.0 - s)).astype(BF)
    weight_grad(0)

    exch_c("recv")
    rows = dot(back, r_c[...].reshape(256, 256)).astype(BF)
    for k in range(nx):
        s_d[k] = rows[k * 32:(k + 1) * 32, :]
    r_d[ix] = s_d[ix]
    exch_d("start")

    for l in range(DEGREES):
        exchange("x", nx, gw_send.at[l], gw_recv.at[l], ws_sem.at[l], wr_sem.at[l], "recv")
    for l in range(DEGREES):
        total = gw_recv[l, 0].astype(F32)
        for k in range(1, nx):
            total = total + gw_recv[l, k].astype(F32)
        sum_x_send[l * 16:(l + 1) * 16, :] = total.astype(BF)
    sum_x[yr] = sum_x_send[...]

    def step_u(d, mode):
        other = (yr + d) % 4
        to = yq * 4 + other
        if mode == "recv":
            remote(sum_x_send, sum_x.at[other], us_sem.at[other], ur_sem.at[other], ix, to).wait_recv()
            return
        copy = remote(sum_x_send, sum_x.at[yr], us_sem.at[other], ur_sem.at[yr], ix, to)
        copy.start() if mode == "start" else copy.wait_send()

    def step_v(d, mode):
        other = (yq + d) % 4
        to = other * 4 + yr
        if mode == "recv":
            remote(sum_x_send, sum_y.at[other], vs_sem.at[other], vr_sem.at[other], ix, to).wait_recv()
            return
        copy = remote(sum_y.at[yq], sum_y.at[yq], vs_sem.at[other], vr_sem.at[yq], ix, to)
        copy.start() if mode == "start" else copy.wait_send()

    def step_o(d, mode):
        other = (ix + d) % nx
        if mode == "recv":
            remote(sum_x_send, out_recv.at[other], os_sem.at[other], or_sem.at[other], other, iy).wait_recv()
            return
        copy = remote(out_recv.at[ix], out_recv.at[ix], os_sem.at[other], or_sem.at[ix], other, iy)
        copy.start() if mode == "start" else copy.wait_send()

    for d in range(1, 4):
        step_u(d, "start")

    exch_d("recv")
    fetched = dot(pick_p[...], r_d[...].reshape(256, 256)).astype(BF)
    keep = jnp.where(iota((16, 256), 0) % 4 == iota((16, 256), 1) // 64, 1.0, 0.0)
    for q in range(8):
        rows16 = fetched[q * 16:(q + 1) * 16, 0:200]
        for r in range(4):
            t = q * 4 + r
            out = dot(rows16, basis[t])
            wanted = keep * jnp.where(iota((16, 256), 0) // 4 == r, 1.0, 0.0)
            dens[t:t + 1, :] = jnp.sum(out * wanted, axis=0, keepdims=True)

    for d in range(1, 4):
        step_u(d, "recv")
    total = sum_x[0].astype(F32)
    for k in range(1, 4):
        total = total + sum_x[k].astype(F32)
    sum_y[yq] = total.astype(BF)
    for d in range(1, 4):
        step_v(d, "start")

    folded = dens[:, 0:128] + dens[:, 128:256]
    tmp256[0:32, :] = folded + pltpu.roll(folded, 64, 1)
    even = tmp256[pl.ds(0, 16, stride=2), :]
    odd_rows = tmp256[pl.ds(1, 16, stride=2), :]
    dens_out[...] = jnp.where(iota((16, 128), 1) < 64, even, odd_rows)

    for d in range(1, 4):
        step_v(d, "recv")
    total = sum_y[0].astype(F32)
    for k in range(1, 4):
        total = total + sum_y[k].astype(F32)
    out_recv[ix] = total.astype(BF)
    for d in range(1, nx):
        step_o(d, "start")
    for d in range(1, nx):
        step_o(d, "recv")
    for l in range(DEGREES):
        for k in range(nx):
            gw_out[l, k * 16:(k + 1) * 16, :] = out_recv[k, l * 16:(l + 1) * 16, :].astype(F32)

    for c in range(len(CHUNKS)):
        for copy in x_copies(c) + y_copies(c):
            copy.wait_send()
    for exch in (exch_a, exch_b, exch_c, exch_d):
        exch("send")
    for l in range(DEGREES):
        exchange("x", nx, gw_send.at[l], gw_recv.at[l], ws_sem.at[l], wr_sem.at[l], "send")
    for d in range(1, 4):
        step_u(d, "send")
        step_v(d, "send")
    for d in range(1, nx):
        step_o(d, "send")


def body(nx, ny, irreps, mix_weight, readout, ghost_x, ghost_y, edge_source_row, edge_dst, radial,
         tile_peer, tile_block, tile_count, basis, density_cot):
    irr = jnp.transpose(irreps[0, 0], (1, 0, 2))
    small = jnp.concatenate(
        [
            ghost_x.reshape(1, 128),
            ghost_y.reshape(1, 128),
            tile_peer.reshape(1, 128),
            tile_block.reshape(1, 128),
            jnp.broadcast_to(tile_count.reshape(32, 1), (32, 4)).reshape(1, 128),
            jnp.zeros((3, 128), jnp.int32),
        ],
        axis=0,
    )
    nch = len(CHUNKS)
    dma = pltpu.SemaphoreType.DMA
    vm = pltpu.VMEM
    dens, gw = pl.pallas_call(
        functools.partial(kernel, nx, ny),
        out_shape=(
            jax.ShapeDtypeStruct((16, 128), F32),
            jax.ShapeDtypeStruct((5, 128, 128), F32),
        ),
        in_specs=[pl.BlockSpec(memory_space=pltpu.VMEM)] * 8 + [pl.BlockSpec(memory_space=pl.ANY)],
        out_specs=(pl.BlockSpec(memory_space=pltpu.VMEM),) * 2,
        scratch_shapes=[
            vm((32, 200, 256), BF),
            vm((25, 256, 128), BF),
            vm((25, 128, 128), BF),
            vm((25, 128, 128), BF),
            vm((128, 128), BF),
            vm((128, 256), BF),
            vm((2048, 384), BF),
            vm((128, 2048), BF),
            vm((640, 2048), BF),
            vm((25, 128, 384), BF),
            vm((25, 128, 128), BF),
            vm((25, 128, 128), F32),
            vm((25, 128, 128), BF),
            vm((128, 128), F32),
            vm((128, 128), F32),
            vm((128, 128), F32),
            vm((128, 128), F32),
            vm((256, 128), F32),
            vm((nx, 32, 256), BF), vm((nx, 32, 256), BF),
            vm((ny, 16, 256), BF), vm((ny, 16, 256), BF),
            vm((ny, 16, 256), BF), vm((ny, 16, 256), BF),
            vm((nx, 32, 256), BF), vm((nx, 32, 256), BF),
            vm((128, 256), BF),
            vm((256, 128), BF),
            vm((32, 256), F32),
            vm((5, nx, 16, 128), BF),
            vm((5, nx, 16, 128), BF),
            vm((80, 128), BF),
            vm((4, 80, 128), BF),
            vm((4, 80, 128), BF),
            vm((nx, 80, 128), BF),
            dma,
            dma((nch, 2)), dma((nch, 2)), dma((nch, 2)), dma((nch, 2)),
            dma((nx,)), dma((nx,)), dma((ny,)), dma((ny,)),
            dma((ny,)), dma((ny,)), dma((nx,)), dma((nx,)),
            dma((5, nx)), dma((5, nx)), dma((4,)), dma((4,)), dma((4,)), dma((4,)), dma((nx,)), dma((nx,)),
        ],
        compiler_params=pltpu.CompilerParams(
            collective_id=0, has_side_effects=True, vmem_limit_bytes=48 * 1024 * 1024
        ),
    )(
        irr,
        mix_weight,
        readout,
        small,
        edge_source_row.reshape(16, 128),
        edge_dst.reshape(16, 128),
        radial.reshape(25, 1, 2048),
        density_cot.reshape(16, 128),
        basis.reshape(32, 200, 256),
    )
    return dens.reshape(1, 1, 2048), gw


def solution(mesh):
    nx, ny = mesh.shape["gx"], mesh.shape["gy"]
    placed = (
        P("gx", "gy", None, None, None),
        P(),
        P(),
        P("gx", "gy", None, None),
        P("gx", "gy", None, None),
        P("gx", "gy", None),
        P("gx", "gy", None),
        P("gx", "gy", None, None),
        P("gx", "gy", None, None),
        P("gx", "gy", None, None),
        P("gx", "gy", None),
        P("gx", "gy", None, None, None),
        P("gx", "gy", None),
    )
    return jax.shard_map(
        functools.partial(body, nx, ny),
        mesh=mesh, in_specs=placed, out_specs=(P("gx", "gy", None), P()), check_vma=False,
    )
```

```python
import functools

import jax
import jax.numpy as jnp
from jax import lax
from jax.experimental import pallas as pl
from jax.experimental.pallas import tpu as pltpu
from jax.sharding import PartitionSpec as P

MESH = pl.DeviceIdType.MESH
BF = jnp.bfloat16
F32 = jnp.float32

CHUNKS = ((0, 1), (4, 6), (6, 9), (16, 20), (20, 25), (9, 13), (13, 16), (1, 4))
DEGREES = 5


def degree_of(m):
    l = 0
    while (l + 1) * (l + 1) <= m:
        l += 1
    return l


def iota(shape, dim):
    return lax.broadcasted_iota(jnp.int32, shape, dim)


def dot(a, b):
    return jnp.dot(a, b, preferred_element_type=F32)


def dot_nt(a, b):
    return lax.dot_general(a, b, (((1,), (1,)), ((), ())), preferred_element_type=F32)


def dot_tn(a, b):
    return lax.dot_general(a, b, (((0,), (0,)), ((), ())), preferred_element_type=F32)


def kernel(
    nx, ny,
    irr_h, w_h, ro_h, gx_h, gy_h, src_h, dst_h, rad_h, peer_h, block_h, count_h, basis_h, cot_h,
    dens_out, gw_out,
    w, ro, gxi, gyi, src, dst, rad, peer, block, count, basis, cot, table, roc, xface, yface, hot_x, hot_y, source_hot, dst_mask, scaled, op,
    y_st, g_st, gg_st, gate, coef, gate_grad, atom_grad, tmp256,
    s_a, r_a, s_b, r_b, s_c, r_c, s_d, r_d, pick_p, own_hot, dens,
    gw_send1, gw_recv1, gw_send2, gw_recv2, sum_y, out_recv,
    in_sem, xs_sem, xr_sem, ys_sem, yr_sem,
    as_sem, ar_sem, bs_sem, br_sem, cs_sem, cr_sem, ds_sem, dr_sem,
    ws_sem, wr_sem, us_sem, ur_sem, os_sem, or_sem,
):
    ix = lax.axis_index("gx")
    iy = lax.axis_index("gy")
    left, right = (ix + nx - 1) % nx, (ix + 1) % nx
    lower, upper = (iy + ny - 1) % ny, (iy + 1) % ny

    local = {}
    for n, (name, held, here) in enumerate((
        ("gxi", gx_h, gxi), ("irr", irr_h, table.at[:, pl.ds(0, 128), :]), ("gyi", gy_h, gyi), ("src", src_h, src), ("dst", dst_h, dst),
        ("rad", rad_h, rad), ("peer", peer_h, peer), ("block", block_h, block), ("count", count_h, count),
        ("cot", cot_h, cot), ("basis", basis_h, basis), ("w", w_h, w), ("ro", ro_h, ro),
    )):
        local[name] = pltpu.make_async_copy(held, here, in_sem.at[n])
        local[name].start()

    def arrive(*names):
        for name in names:
            local[name].wait()

    barrier = pltpu.get_barrier_semaphore()

    def greet_x(d, c):
        pl.semaphore_signal(barrier, inc=1, device_id=((ix + d) % nx, iy), device_id_type=MESH)
        return c

    def greet_y(d, c):
        pl.semaphore_signal(barrier, inc=1, device_id=(ix, (iy + d) % ny), device_id_type=MESH)
        return c

    lax.fori_loop(1, nx, greet_x, 0)
    lax.fori_loop(1, ny, greet_y, 0)

    def remote(s, d, ssem, rsem, i, j):
        return pltpu.make_async_remote_copy(
            src_ref=s, dst_ref=d, send_sem=ssem, recv_sem=rsem, device_id=(i, j), device_id_type=MESH
        )

    def x_copies(c):
        lo, hi = CHUNKS[c]
        n = hi - lo
        return (
            remote(xface.at[pl.ds(lo, n), pl.ds(64, 64), :], table.at[pl.ds(lo, n), pl.ds(128, 64), :],
                   xs_sem.at[c, 0], xr_sem.at[c, 0], right, iy),
            remote(xface.at[pl.ds(lo, n), pl.ds(0, 64), :], table.at[pl.ds(lo, n), pl.ds(192, 64), :],
                   xs_sem.at[c, 1], xr_sem.at[c, 1], left, iy),
        )

    def y_copies(c):
        lo, hi = CHUNKS[c]
        n = hi - lo
        return (
            remote(yface.at[pl.ds(lo, n), pl.ds(64, 64), :], table.at[pl.ds(lo, n), pl.ds(256, 64), :],
                   ys_sem.at[c, 0], yr_sem.at[c, 0], ix, upper),
            remote(yface.at[pl.ds(lo, n), pl.ds(0, 64), :], table.at[pl.ds(lo, n), pl.ds(320, 64), :],
                   ys_sem.at[c, 1], yr_sem.at[c, 1], ix, lower),
        )

    def ghost_row(ref):
        return jnp.concatenate([ref[0:1, :], ref[1:2, :]], axis=1)

    arrive("gxi")
    hot_x[...] = jnp.where(iota((128, 128), 0) == ghost_row(gxi), 1.0, 0.0).T.astype(BF)
    arrive("irr")

    chooser = hot_x[...]
    for lo, hi in CHUNKS:
        for m in range(lo, hi):
            xface[m] = dot(chooser, table[m, 0:128, :]).astype(BF)

    arrive("gyi")
    gy_row = ghost_row(gyi)
    for half in range(2):
        hot_y[:, half * 128:(half + 1) * 128] = (
            jnp.where(iota((128, 128), 0) + half * 128 == gy_row, 1.0, 0.0).T.astype(BF)
        )

    def send_y(c):
        for copy in x_copies(c):
            copy.wait_recv()
        lo, hi = CHUNKS[c]
        for m in range(lo, hi):
            yface[m] = dot(hot_y[...], table[m, 0:256, :]).astype(BF)
        for copy in y_copies(c):
            copy.start()

    arrive("src", "dst", "rad")
    src_cols = jnp.concatenate([src[...].astype(F32), jnp.zeros((112, 128), F32)], axis=0).T
    lane384 = iota((128, 384), 1).astype(F32)
    sub128 = iota((128, 128), 0)
    for k in range(16):
        source_hot[k * 128:(k + 1) * 128, :] = jnp.where(src_cols[:, k:k + 1] == lane384, 1.0, 0.0).astype(BF)
        dst_mask[:, k * 128:(k + 1) * 128] = jnp.where(sub128 == dst[k:k + 1, :], 1.0, 0.0).astype(BF)

    def build_op(c):
        lo, hi = CHUNKS[c]
        n = hi - lo
        for i in range(n):
            row = rad[lo + i].astype(BF)
            scaled[i * 128:(i + 1) * 128, :] = dst_mask[...] * jnp.broadcast_to(row, (128, 2048))
        built = dot(scaled[0:n * 128, :], source_hot[...])
        for i in range(n):
            op[lo + i] = built[i * 128:(i + 1) * 128, :].astype(BF)

    arrive("peer", "block", "count", "cot")

    def slot_row(ref):
        return jnp.concatenate([ref[k:k + 1, :] for k in range(4)], axis=1)

    peer_row = slot_row(peer)
    same = (jnp.broadcast_to(peer_row, (128, 128)).astype(F32).T == peer_row.astype(F32)) & (
        iota((128, 128), 0) < iota((128, 128), 1)
    )
    rank = jnp.sum(jnp.where(same, 1.0, 0.0), axis=0, keepdims=True).astype(jnp.int32)
    live_row = (iota((1, 128), 1) // 32) < jnp.concatenate([count[...]] * 4, axis=1)
    position = jnp.where(live_row, peer_row * 2 + rank, -1)
    chosen = jnp.where(iota((256, 128), 0) == position, 1.0, 0.0)
    slot_n = iota((128, 128), 0)
    reorder = jnp.where(iota((128, 128), 1) == slot_n % 4 * 32 + slot_n // 4, 1.0, 0.0).astype(BF)
    for half in range(2):
        pick_p[:, half * 128:(half + 1) * 128] = dot_nt(
            reorder, chosen[half * 128:(half + 1) * 128, :].astype(BF)
        ).astype(BF)
    cot_f = cot[...].astype(F32)
    cot_rows = jnp.concatenate([cot_f[:, u * 128:(u + 1) * 128] for u in range(16)], axis=0).astype(BF)
    tile_n = slot_n % 32
    spread = jnp.where(iota((128, 16), 1) == iota((128, 16), 0) % 32 // 2, 1.0, 0.0).astype(BF)
    picked = dot(spread, cot_rows)
    mine = jnp.where((iota((128, 128), 1) // 64) == tile_n % 2, picked, pltpu.roll(picked, 64, 1))
    both = jnp.concatenate([mine, mine], axis=1)
    weights = jnp.where(iota((128, 256), 1) // 64 == iota((128, 256), 0) // 32, both, 0.0)

    weights_t = jnp.concatenate([weights[:, 0:128].T, weights[:, 128:256].T], axis=0).astype(BF)
    arrive("basis")

    lane_tile = iota((200, 128), 1) % 32

    slot_grad = jnp.zeros((200, 128), F32)
    for t in range(32):
        slot_grad = jnp.where(lane_tile == t, dot(basis[t], weights_t), slot_grad)
    id_rows = jnp.where(iota((56, 128), 0) == 0, jnp.broadcast_to(slot_row(block).astype(F32), (56, 128)), 0.0)
    tmp256[...] = jnp.concatenate([slot_grad, id_rows], axis=0)
    sent = dot_nt(chosen.astype(BF), tmp256[...].astype(BF)).astype(BF)
    for k in range(nx):
        s_a[k] = sent[k * 32:(k + 1) * 32, :]
    r_a[ix] = s_a[ix]

    def exchange(axis, n, s, r, ssem, rsem, mode):
        me = ix if axis == "x" else iy
        if mode != "start":
            to = (right, iy) if axis == "x" else (ix, upper)
            everything = remote(r.at[pl.ds(0, n - 1)], r.at[pl.ds(0, n - 1)], ssem, rsem, *to)
            everything.wait_recv() if mode == "recv" else everything.wait_send()
            return
        for d in range(1, n):
            other = (me + d) % n
            to = (other, iy) if axis == "x" else (ix, other)
            remote(s(other), r.at[me], ssem, rsem, *to).start()

    def slot_of(ref):
        return lambda k: ref.at[k]

    exch_a = functools.partial(exchange, "x", nx, slot_of(s_a), r_a, as_sem.at[0], ar_sem.at[0])
    exch_b = functools.partial(exchange, "y", ny, slot_of(s_b), r_b, bs_sem.at[0], br_sem.at[0])
    exch_c = functools.partial(exchange, "y", ny, slot_of(s_c), r_c, cs_sem.at[0], cr_sem.at[0])
    exch_d = functools.partial(exchange, "x", nx, slot_of(s_d), r_d, ds_sem.at[0], dr_sem.at[0])
    exch_g1 = functools.partial(exchange, "x", nx, slot_of(gw_send1), gw_recv1, ws_sem.at[0], wr_sem.at[0])
    exch_g2 = functools.partial(exchange, "x", nx, slot_of(gw_send2), gw_recv2, ws_sem.at[1], wr_sem.at[1])
    exch_u = functools.partial(exchange, "y", ny, lambda k: sum_y.at[iy], sum_y, us_sem.at[0], ur_sem.at[0])
    exch_o = functools.partial(exchange, "x", nx, lambda k: out_recv.at[ix], out_recv, os_sem.at[0], or_sem.at[0])

    pl.semaphore_wait(barrier, nx + ny - 2)
    for c in range(len(CHUNKS)):
        for copy in x_copies(c):
            copy.start()
    exch_a("start")

    build_op(0)
    build_op(1)
    build_op(2)
    send_y(0)
    send_y(1)
    build_op(3)
    send_y(2)
    send_y(3)
    build_op(4)
    send_y(4)
    send_y(5)
    send_y(6)
    send_y(7)

    n_i, n_j = iota((256, 256), 0), iota((256, 256), 1)
    turned = (n_i % 16) // 2 * 32 + n_i // 16 * 2 + n_i % 2
    turn = jnp.where(n_j == turned, 1.0, 0.0).astype(BF)
    back = jnp.where(n_j == n_i % 32 // 2 * 16 + n_i // 32 * 2 + n_i % 2, 1.0, 0.0).astype(BF)
    exch_a("recv")
    rows = dot(turn, r_a[...].reshape(256, 256)).astype(BF)
    for k in range(ny):
        s_b[k] = rows[k * 16:(k + 1) * 16, :]
    r_b[iy] = s_b[iy]
    exch_b("start")

    build_op(5)
    build_op(6)
    build_op(7)

    arrive("w", "ro")
    ro_f = ro[...].astype(F32)
    ro_cols = jnp.concatenate([ro_f, jnp.zeros((103, 128), F32)], axis=0).T
    lane128 = iota((128, 128), 1)
    coef[...] = jnp.zeros((128, 128), F32)
    for m in range(25):
        roc[m * 128:(m + 1) * 128, :] = jnp.where(lane128 == m, ro_cols, 0.0).astype(BF)

    def forward(c):
        for copy in y_copies(c):
            copy.wait_recv()
        lo, hi = CHUNKS[c]
        ys = [dot(op[m], table[m]).astype(BF) for m in range(lo, hi)]
        gs = [dot(y, w[degree_of(lo + i)]) for i, y in enumerate(ys)]
        if lo == 0:
            gate[...] = jax.nn.sigmoid(gs[0])
        for i, (y, g) in enumerate(zip(ys, gs)):
            y_st[lo + i] = y
            g_st[lo + i] = g
        s = gate[...]
        updated = [(table[lo + i, 0:128, :].astype(F32) + s * g).astype(BF) for i, g in enumerate(gs)]
        wide = updated[0] if len(updated) == 1 else jnp.concatenate(updated, axis=1)
        coef[...] += dot(wide, roc[lo * 128:hi * 128, :])

    def backward(c):
        lo, hi = CHUNKS[c]
        total = gate_grad[...]
        ag = atom_grad[...]
        for m in range(lo, hi):
            gu = ag[:, m:m + 1] * ro_f[m:m + 1, :]
            total = total + gu * g_st[m]
            if m > 0:
                gg_st[m] = (gu * gate[...]).astype(BF)
        gate_grad[...] = total

    def weight_grad(l, held, at):
        lo, hi = l * l, (l + 1) * (l + 1)
        n = (hi - lo) * 128
        part = dot_tn(y_st[lo:hi].reshape(n, 128), gg_st[lo:hi].reshape(n, 128)).astype(BF)
        for k in range(nx):
            held[k, at * 16:(at + 1) * 16, :] = part[k * 16:(k + 1) * 16, :]

    forward(0)
    forward(1)

    exch_b("recv")
    incoming = r_b[...].reshape(256, 256)
    ids = incoming[:, 128:256].astype(F32)[:, 72:73]
    owner = jnp.where(ids == iota((256, 128), 1).astype(F32), 1.0, 0.0)
    own_hot[...] = owner.astype(BF)
    owner_t = jnp.concatenate([owner[0:128, :].T[0:16, :], owner[128:256, :].T[0:16, :]], axis=1).astype(BF)
    block_grad = dot(owner_t, incoming)
    for j in range(8):
        moved = block_grad if j == 0 else pltpu.roll(block_grad, 256 - 25 * j, 1)
        atom_grad[pl.ds(j, 16, stride=8), :] = moved[:, 0:128]
    gate_grad[...] = jnp.zeros((128, 128), F32)

    backward(0)
    backward(1)
    forward(2)
    backward(2)
    weight_grad(2, gw_send1, 0)
    forward(3)
    backward(3)
    forward(4)
    backward(4)
    weight_grad(4, gw_send1, 1)
    forward(5)
    backward(5)
    forward(6)
    backward(6)
    weight_grad(3, gw_send1, 2)
    gw_recv1[ix] = gw_send1[ix]
    exch_g1("start")
    exch_a("send")
    exch_b("send")
    for c in range(len(CHUNKS)):
        for copy in x_copies(c):
            copy.wait_send()
    forward(7)
    backward(7)
    weight_grad(1, gw_send2, 1)
    gu = atom_grad[:, 0:1] * ro_f[0:1, :]
    s = gate[...]
    gg_st[0] = (gu * s + gate_grad[...] * s * (1.0 - s)).astype(BF)
    weight_grad(0, gw_send2, 0)
    gw_recv2[ix] = gw_send2[ix]
    exch_g2("start")

    coef_rows = jnp.zeros((16, 256), F32)
    valid = jnp.where(iota((16, 256), 1) < 25, 1.0, 0.0)
    for j in range(8):
        part = jnp.concatenate([coef[pl.ds(j, 16, stride=8), :], jnp.zeros((16, 128), F32)], axis=1) * valid
        coef_rows = coef_rows + (part if j == 0 else pltpu.roll(part, 25 * j, 1))
    coef_pad = jnp.concatenate([coef_rows, jnp.zeros((112, 256), F32)], axis=0).astype(BF)
    answer = dot(own_hot[...], coef_pad).astype(BF)
    for k in range(ny):
        s_c[k] = answer[k * 16:(k + 1) * 16, :]
    r_c[iy] = s_c[iy]
    exch_c("start")

    def total_of(ref, n):
        total = ref[0].astype(F32)
        for k in range(1, n):
            total = total + ref[k].astype(F32)
        return total

    exch_g1("recv")
    first = total_of(gw_recv1, nx)
    exch_g2("recv")
    second = total_of(gw_recv2, nx)
    sum_y[iy] = jnp.concatenate([second, first], axis=0).astype(BF)
    exch_u("start")

    exch_c("recv")
    rows = dot(back, r_c[...].reshape(256, 256)).astype(BF)
    for k in range(nx):
        s_d[k] = rows[k * 32:(k + 1) * 32, :]
    r_d[ix] = s_d[ix]
    exch_d("start")

    for c in range(len(CHUNKS)):
        for copy in y_copies(c):
            copy.wait_send()
    exch_c("send")
    exch_g1("send")
    exch_g2("send")

    exch_u("recv")
    out_recv[ix] = total_of(sum_y, ny).astype(BF)
    exch_o("start")

    exch_d("recv")
    fetched = dot(pick_p[...], r_d[...].reshape(256, 256)).astype(BF)
    keep = jnp.where(iota((16, 256), 0) % 4 == iota((16, 256), 1) // 64, 1.0, 0.0)
    for q in range(8):
        rows16 = fetched[q * 16:(q + 1) * 16, 0:200]
        for r in range(4):
            t = q * 4 + r
            out = dot(rows16, basis[t])
            wanted = keep * jnp.where(iota((16, 256), 0) // 4 == r, 1.0, 0.0)
            dens[t:t + 1, :] = jnp.sum(out * wanted, axis=0, keepdims=True)
    folded = dens[:, 0:128] + dens[:, 128:256]
    tmp256[0:32, :] = folded + pltpu.roll(folded, 64, 1)
    even = tmp256[pl.ds(0, 16, stride=2), :]
    odd_rows = tmp256[pl.ds(1, 16, stride=2), :]
    dens_out[...] = jnp.where(iota((16, 128), 1) < 64, even, odd_rows)

    exch_d("send")
    exch_u("send")
    exch_o("recv")
    for at, l in enumerate((0, 1, 2, 4, 3)):
        for k in range(nx):
            gw_out[l, k * 16:(k + 1) * 16, :] = out_recv[k, at * 16:(at + 1) * 16, :].astype(F32)
    exch_o("send")


def body(nx, ny, irreps, mix_weight, readout, ghost_x, ghost_y, edge_source_row, edge_dst, radial,
         tile_peer, tile_block, tile_count, basis, density_cot):
    irr = jnp.transpose(irreps[0, 0], (1, 0, 2))
    nch = len(CHUNKS)
    dma = pltpu.SemaphoreType.DMA
    vm = pltpu.VMEM
    dens, gw = pl.pallas_call(
        functools.partial(kernel, nx, ny),
        out_shape=(
            jax.ShapeDtypeStruct((16, 128), F32),
            jax.ShapeDtypeStruct((5, 128, 128), F32),
        ),
        in_specs=[pl.BlockSpec(memory_space=pltpu.HBM)] * 13,
        out_specs=(pl.BlockSpec(memory_space=pltpu.VMEM),) * 2,
        scratch_shapes=[
            vm((5, 128, 128), BF),
            vm((25, 128), BF),
            vm((2, 64), jnp.int32), vm((2, 64), jnp.int32),
            vm((16, 128), jnp.int32), vm((16, 128), jnp.int32),
            vm((25, 1, 2048), F32),
            vm((4, 32), jnp.int32), vm((4, 32), jnp.int32), vm((1, 32), jnp.int32),
            vm((32, 200, 256), BF),
            vm((1, 2048), BF),
            vm((25, 384, 128), BF),
            vm((3200, 128), BF),
            vm((25, 128, 128), BF),
            vm((25, 128, 128), BF),
            vm((128, 128), BF),
            vm((128, 256), BF),
            vm((2048, 384), BF),
            vm((128, 2048), BF),
            vm((640, 2048), BF),
            vm((25, 128, 384), BF),
            vm((25, 128, 128), BF),
            vm((25, 128, 128), F32),
            vm((25, 128, 128), BF),
            vm((128, 128), F32),
            vm((128, 128), F32),
            vm((128, 128), F32),
            vm((128, 128), F32),
            vm((256, 128), F32),
            vm((nx, 32, 256), BF), vm((nx, 32, 256), BF),
            vm((ny, 16, 256), BF), vm((ny, 16, 256), BF),
            vm((ny, 16, 256), BF), vm((ny, 16, 256), BF),
            vm((nx, 32, 256), BF), vm((nx, 32, 256), BF),
            vm((128, 256), BF),
            vm((256, 128), BF),
            vm((32, 256), F32),
            vm((nx, 48, 128), BF), vm((nx, 48, 128), BF),
            vm((nx, 32, 128), BF), vm((nx, 32, 128), BF),
            vm((ny, 80, 128), BF),
            vm((nx, 80, 128), BF),
            dma((13,)),
            dma((nch, 2)), dma((nch, 2)), dma((nch, 2)), dma((nch, 2)),
            dma((1,)), dma((1,)), dma((1,)), dma((1,)), dma((1,)), dma((1,)), dma((1,)), dma((1,)),
            dma((2,)), dma((2,)), dma((1,)), dma((1,)), dma((1,)), dma((1,)),
        ],
        compiler_params=pltpu.CompilerParams(
            collective_id=0, has_side_effects=True, vmem_limit_bytes=60 * 1024 * 1024
        ),
    )(
        irr,
        mix_weight,
        readout,
        ghost_x.reshape(2, 64),
        ghost_y.reshape(2, 64),
        edge_source_row.reshape(16, 128),
        edge_dst.reshape(16, 128),
        radial.reshape(25, 1, 2048),
        jnp.transpose(tile_peer[0, 0]),
        jnp.transpose(tile_block[0, 0]),
        tile_count.reshape(1, 32),
        basis.reshape(32, 200, 256),
        density_cot.reshape(1, 2048),
    )
    return dens.reshape(1, 1, 2048), gw


def solution(mesh):
    nx, ny = mesh.shape["gx"], mesh.shape["gy"]
    placed = (
        P("gx", "gy", None, None, None),
        P(),
        P(),
        P("gx", "gy", None, None),
        P("gx", "gy", None, None),
        P("gx", "gy", None),
        P("gx", "gy", None),
        P("gx", "gy", None, None),
        P("gx", "gy", None, None),
        P("gx", "gy", None, None),
        P("gx", "gy", None),
        P("gx", "gy", None, None, None),
        P("gx", "gy", None),
    )
    return jax.shard_map(
        functools.partial(body, nx, ny),
        mesh=mesh, in_specs=placed, out_specs=(P("gx", "gy", None), P()), check_vma=False,
    )
```

```python
import functools

import jax
import jax.numpy as jnp
from jax import lax
from jax.experimental import pallas as pl
from jax.experimental.pallas import tpu as pltpu
from jax.sharding import PartitionSpec as P

MESH = pl.DeviceIdType.MESH
BF = jnp.bfloat16
F32 = jnp.float32

CHUNKS = ((0, 1), (4, 6), (6, 9), (16, 20), (20, 25), (9, 13), (13, 16), (1, 4))
DEGREES = 5


def degree_of(m):
    l = 0
    while (l + 1) * (l + 1) <= m:
        l += 1
    return l


def iota(shape, dim):
    return lax.broadcasted_iota(jnp.int32, shape, dim)


def dot(a, b):
    return jnp.dot(a, b, preferred_element_type=F32)


def dot_nt(a, b):
    return lax.dot_general(a, b, (((1,), (1,)), ((), ())), preferred_element_type=F32)


def dot_tn(a, b):
    return lax.dot_general(a, b, (((0,), (0,)), ((), ())), preferred_element_type=F32)


def kernel(
    nx, ny,
    irr_h, w_h, ro_h, gx_h, gy_h, src_h, dst_h, rad_h, peer_h, block_h, count_h, basis_h, cot_h,
    dens_out, out_recv2, out_recv1,
    w, ro, gxi, gyi, src, dst, rad, peer, block, count, basis, cot, table, roc, xface, yface, hot_x, hot_y, source_hot, dst_mask, scaled, op,
    y_st, g_st, gg_st, gate, coef, gate_grad, atom_grad, tmp256,
    s_a, r_a, s_b, r_b, s_c, r_c, s_d, r_d, pick_p, own_hot, dens,
    gw_send1, gw_recv1, gw_send2, gw_recv2, sum_y1, sum_y2,
    in_sem, xs_sem, xr_sem, ys_sem, yr_sem,
    as_sem, ar_sem, bs_sem, br_sem, cs_sem, cr_sem, ds_sem, dr_sem,
    ws_sem, wr_sem, us_sem, ur_sem, os_sem, or_sem,
):
    ix = lax.axis_index("gx")
    iy = lax.axis_index("gy")
    left, right = (ix + nx - 1) % nx, (ix + 1) % nx
    lower, upper = (iy + ny - 1) % ny, (iy + 1) % ny

    local = {}
    for n, (name, held, here) in enumerate((
        ("gxi", gx_h, gxi), ("irr", irr_h, table.at[:, pl.ds(0, 128), :]), ("gyi", gy_h, gyi), ("src", src_h, src), ("dst", dst_h, dst),
        ("rad", rad_h, rad), ("peer", peer_h, peer), ("block", block_h, block), ("count", count_h, count),
        ("cot", cot_h, cot), ("basis", basis_h, basis), ("w", w_h, w), ("ro", ro_h, ro),
    )):
        local[name] = pltpu.make_async_copy(held, here, in_sem.at[n])
        local[name].start()

    def arrive(*names):
        for name in names:
            local[name].wait()

    barrier = pltpu.get_barrier_semaphore()

    def greet_x(d, c):
        pl.semaphore_signal(barrier, inc=1, device_id=((ix + d) % nx, iy), device_id_type=MESH)
        return c

    def greet_y(d, c):
        pl.semaphore_signal(barrier, inc=1, device_id=(ix, (iy + d) % ny), device_id_type=MESH)
        return c

    lax.fori_loop(1, nx, greet_x, 0)
    lax.fori_loop(1, ny, greet_y, 0)

    def remote(s, d, ssem, rsem, i, j):
        return pltpu.make_async_remote_copy(
            src_ref=s, dst_ref=d, send_sem=ssem, recv_sem=rsem, device_id=(i, j), device_id_type=MESH
        )

    def x_copies(c):
        lo, hi = CHUNKS[c]
        n = hi - lo
        return (
            remote(xface.at[pl.ds(lo, n), pl.ds(64, 64), :], table.at[pl.ds(lo, n), pl.ds(128, 64), :],
                   xs_sem.at[c, 0], xr_sem.at[c, 0], right, iy),
            remote(xface.at[pl.ds(lo, n), pl.ds(0, 64), :], table.at[pl.ds(lo, n), pl.ds(192, 64), :],
                   xs_sem.at[c, 1], xr_sem.at[c, 1], left, iy),
        )

    def y_copies(c):
        lo, hi = CHUNKS[c]
        n = hi - lo
        return (
            remote(yface.at[pl.ds(lo, n), pl.ds(64, 64), :], table.at[pl.ds(lo, n), pl.ds(256, 64), :],
                   ys_sem.at[c, 0], yr_sem.at[c, 0], ix, upper),
            remote(yface.at[pl.ds(lo, n), pl.ds(0, 64), :], table.at[pl.ds(lo, n), pl.ds(320, 64), :],
                   ys_sem.at[c, 1], yr_sem.at[c, 1], ix, lower),
        )

    def ghost_row(ref):
        return jnp.concatenate([ref[0:1, :], ref[1:2, :]], axis=1)

    arrive("gxi")
    hot_x[...] = jnp.where(iota((128, 128), 0) == ghost_row(gxi), 1.0, 0.0).T.astype(BF)
    arrive("irr")

    chooser = hot_x[...]
    for lo, hi in CHUNKS:
        for m in range(lo, hi):
            xface[m] = dot(chooser, table[m, 0:128, :]).astype(BF)

    arrive("gyi")
    gy_row = ghost_row(gyi)
    for half in range(2):
        hot_y[:, half * 128:(half + 1) * 128] = (
            jnp.where(iota((128, 128), 0) + half * 128 == gy_row, 1.0, 0.0).T.astype(BF)
        )

    def send_y(c):
        for copy in x_copies(c):
            copy.wait_recv()
        lo, hi = CHUNKS[c]
        for m in range(lo, hi):
            yface[m] = dot(hot_y[...], table[m, 0:256, :]).astype(BF)
        for copy in y_copies(c):
            copy.start()

    arrive("src", "dst", "rad")
    src_cols = jnp.concatenate([src[...].astype(F32), jnp.zeros((112, 128), F32)], axis=0).T
    lane384 = iota((128, 384), 1).astype(F32)
    sub128 = iota((128, 128), 0)
    for k in range(16):
        source_hot[k * 128:(k + 1) * 128, :] = jnp.where(src_cols[:, k:k + 1] == lane384, 1.0, 0.0).astype(BF)
        dst_mask[:, k * 128:(k + 1) * 128] = jnp.where(sub128 == dst[k:k + 1, :], 1.0, 0.0).astype(BF)

    def build_op(c):
        lo, hi = CHUNKS[c]
        n = hi - lo
        for i in range(n):
            row = rad[lo + i].astype(BF)
            scaled[i * 128:(i + 1) * 128, :] = dst_mask[...] * jnp.broadcast_to(row, (128, 2048))
        built = dot(scaled[0:n * 128, :], source_hot[...])
        for i in range(n):
            op[lo + i] = built[i * 128:(i + 1) * 128, :].astype(BF)

    arrive("peer", "block", "count", "cot")

    def slot_row(ref):
        return jnp.concatenate([ref[k:k + 1, :] for k in range(4)], axis=1)

    peer_row = slot_row(peer)
    same = (jnp.broadcast_to(peer_row, (128, 128)).astype(F32).T == peer_row.astype(F32)) & (
        iota((128, 128), 0) < iota((128, 128), 1)
    )
    rank = jnp.sum(jnp.where(same, 1.0, 0.0), axis=0, keepdims=True).astype(jnp.int32)
    live_row = (iota((1, 128), 1) // 32) < jnp.concatenate([count[...]] * 4, axis=1)
    position = jnp.where(live_row, peer_row * 2 + rank, -1)
    chosen = jnp.where(iota((256, 128), 0) == position, 1.0, 0.0)
    slot_n = iota((128, 128), 0)
    reorder = jnp.where(iota((128, 128), 1) == slot_n % 4 * 32 + slot_n // 4, 1.0, 0.0).astype(BF)
    for half in range(2):
        pick_p[:, half * 128:(half + 1) * 128] = dot_nt(
            reorder, chosen[half * 128:(half + 1) * 128, :].astype(BF)
        ).astype(BF)
    cot_f = cot[...].astype(F32)
    cot_rows = jnp.concatenate([cot_f[:, u * 128:(u + 1) * 128] for u in range(16)], axis=0).astype(BF)
    tile_n = slot_n % 32
    spread = jnp.where(iota((128, 16), 1) == iota((128, 16), 0) % 32 // 2, 1.0, 0.0).astype(BF)
    picked = dot(spread, cot_rows)
    mine = jnp.where((iota((128, 128), 1) // 64) == tile_n % 2, picked, pltpu.roll(picked, 64, 1))
    both = jnp.concatenate([mine, mine], axis=1)
    weights = jnp.where(iota((128, 256), 1) // 64 == iota((128, 256), 0) // 32, both, 0.0)

    weights_t = jnp.concatenate([weights[:, 0:128].T, weights[:, 128:256].T], axis=0).astype(BF)
    arrive("basis")

    lane_tile = iota((200, 128), 1) % 32

    slot_grad = jnp.zeros((200, 128), F32)
    for t in range(32):
        slot_grad = jnp.where(lane_tile == t, dot(basis[t], weights_t), slot_grad)
    id_rows = jnp.where(iota((56, 128), 0) == 0, jnp.broadcast_to(slot_row(block).astype(F32), (56, 128)), 0.0)
    tmp256[...] = jnp.concatenate([slot_grad, id_rows], axis=0)
    sent = dot_nt(chosen.astype(BF), tmp256[...].astype(BF)).astype(BF)
    for k in range(nx):
        s_a[k] = sent[k * 32:(k + 1) * 32, :]
    r_a[ix] = s_a[ix]

    def exchange(axis, n, s, r, ssem, rsem, mode):
        me = ix if axis == "x" else iy
        if mode != "start":
            to = (right, iy) if axis == "x" else (ix, upper)
            everything = remote(r.at[pl.ds(0, n - 1)], r.at[pl.ds(0, n - 1)], ssem, rsem, *to)
            everything.wait_recv() if mode == "recv" else everything.wait_send()
            return
        for d in range(1, n):
            other = (me + d) % n
            to = (other, iy) if axis == "x" else (ix, other)
            remote(s(other), r.at[me], ssem, rsem, *to).start()

    def slot_of(ref):
        return lambda k: ref.at[k]

    exch_a = functools.partial(exchange, "x", nx, slot_of(s_a), r_a, as_sem.at[0], ar_sem.at[0])
    exch_b = functools.partial(exchange, "y", ny, slot_of(s_b), r_b, bs_sem.at[0], br_sem.at[0])
    exch_c = functools.partial(exchange, "y", ny, slot_of(s_c), r_c, cs_sem.at[0], cr_sem.at[0])
    exch_d = functools.partial(exchange, "x", nx, slot_of(s_d), r_d, ds_sem.at[0], dr_sem.at[0])
    exch_g1 = functools.partial(exchange, "x", nx, slot_of(gw_send1), gw_recv1, ws_sem.at[0], wr_sem.at[0])
    exch_g2 = functools.partial(exchange, "x", nx, slot_of(gw_send2), gw_recv2, ws_sem.at[1], wr_sem.at[1])
    exch_u1 = functools.partial(exchange, "y", ny, lambda k: sum_y1.at[iy], sum_y1, us_sem.at[0], ur_sem.at[0])
    exch_u2 = functools.partial(exchange, "y", ny, lambda k: sum_y2.at[iy], sum_y2, us_sem.at[1], ur_sem.at[1])
    exch_o1 = functools.partial(exchange, "x", nx, lambda k: out_recv1.at[ix], out_recv1, os_sem.at[0], or_sem.at[0])
    exch_o2 = functools.partial(exchange, "x", nx, lambda k: out_recv2.at[ix], out_recv2, os_sem.at[1], or_sem.at[1])

    pl.semaphore_wait(barrier, nx + ny - 2)
    for c in range(len(CHUNKS)):
        for copy in x_copies(c):
            copy.start()
        if c == 2:
            exch_a("start")

    build_op(0)
    build_op(1)
    build_op(2)
    send_y(0)
    send_y(1)
    build_op(3)
    send_y(2)
    send_y(3)
    build_op(4)
    send_y(4)

    n_i, n_j = iota((256, 256), 0), iota((256, 256), 1)
    turned = (n_i % 16) // 2 * 32 + n_i // 16 * 2 + n_i % 2
    turn = jnp.where(n_j == turned, 1.0, 0.0).astype(BF)
    back = jnp.where(n_j == n_i % 32 // 2 * 16 + n_i // 32 * 2 + n_i % 2, 1.0, 0.0).astype(BF)
    exch_a("recv")
    rows = dot(turn, r_a[...].reshape(256, 256)).astype(BF)
    for k in range(ny):
        s_b[k] = rows[k * 16:(k + 1) * 16, :]
    r_b[iy] = s_b[iy]
    exch_b("start")

    send_y(5)
    send_y(6)
    send_y(7)

    build_op(5)
    build_op(6)
    build_op(7)

    arrive("w", "ro")
    ro_f = ro[...].astype(F32)
    ro_cols = jnp.concatenate([ro_f, jnp.zeros((103, 128), F32)], axis=0).T
    lane128 = iota((128, 128), 1)
    coef[...] = jnp.zeros((128, 128), F32)
    for m in range(25):
        roc[m * 128:(m + 1) * 128, :] = jnp.where(lane128 == m, ro_cols, 0.0).astype(BF)

    def forward(c):
        for copy in y_copies(c):
            copy.wait_recv()
        lo, hi = CHUNKS[c]
        ys = [dot(op[m], table[m]).astype(BF) for m in range(lo, hi)]
        gs = [dot(y, w[degree_of(lo + i)]) for i, y in enumerate(ys)]
        if lo == 0:
            gate[...] = jax.nn.sigmoid(gs[0])
        for i, (y, g) in enumerate(zip(ys, gs)):
            y_st[lo + i] = y
            g_st[lo + i] = g
        s = gate[...]
        updated = [(table[lo + i, 0:128, :].astype(F32) + s * g).astype(BF) for i, g in enumerate(gs)]
        wide = updated[0] if len(updated) == 1 else jnp.concatenate(updated, axis=1)
        coef[...] += dot(wide, roc[lo * 128:hi * 128, :])

    def backward(c):
        lo, hi = CHUNKS[c]
        total = gate_grad[...]
        ag = atom_grad[...]
        for m in range(lo, hi):
            gu = ag[:, m:m + 1] * ro_f[m:m + 1, :]
            total = total + gu * g_st[m]
            if m > 0:
                gg_st[m] = (gu * gate[...]).astype(BF)
        gate_grad[...] = total

    def weight_grad(l, held, at):
        lo, hi = l * l, (l + 1) * (l + 1)
        n = (hi - lo) * 128
        part = dot_tn(y_st[lo:hi].reshape(n, 128), gg_st[lo:hi].reshape(n, 128)).astype(BF)
        for k in range(nx):
            held[k, at * 16:(at + 1) * 16, :] = part[k * 16:(k + 1) * 16, :]

    forward(0)
    forward(1)
    forward(2)
    forward(3)
    forward(4)

    exch_b("recv")
    incoming = r_b[...].reshape(256, 256)
    ids = incoming[:, 128:256].astype(F32)[:, 72:73]
    owner = jnp.where(ids == iota((256, 128), 1).astype(F32), 1.0, 0.0)
    own_hot[...] = owner.astype(BF)
    owner_t = jnp.concatenate([owner[0:128, :].T[0:16, :], owner[128:256, :].T[0:16, :]], axis=1).astype(BF)
    block_grad = dot(owner_t, incoming)
    for j in range(8):
        moved = block_grad if j == 0 else pltpu.roll(block_grad, 256 - 25 * j, 1)
        atom_grad[pl.ds(j, 16, stride=8), :] = moved[:, 0:128]
    gate_grad[...] = jnp.zeros((128, 128), F32)

    for c in range(5):
        backward(c)
    weight_grad(2, gw_send1, 0)
    weight_grad(4, gw_send1, 1)
    forward(5)
    backward(5)
    exch_a("send")
    exch_b("send")
    for c in range(len(CHUNKS)):
        for copy in x_copies(c):
            copy.wait_send()
    forward(6)
    backward(6)
    weight_grad(3, gw_send1, 2)
    gw_recv1[ix] = gw_send1[ix]
    exch_g1("start")
    forward(7)
    backward(7)
    weight_grad(1, gw_send2, 1)
    gu = atom_grad[:, 0:1] * ro_f[0:1, :]
    s = gate[...]
    gg_st[0] = (gu * s + gate_grad[...] * s * (1.0 - s)).astype(BF)
    weight_grad(0, gw_send2, 0)
    gw_recv2[ix] = gw_send2[ix]
    exch_g2("start")

    coef_rows = jnp.zeros((16, 256), F32)
    valid = jnp.where(iota((16, 256), 1) < 25, 1.0, 0.0)
    for j in range(8):
        part = jnp.concatenate([coef[pl.ds(j, 16, stride=8), :], jnp.zeros((16, 128), F32)], axis=1) * valid
        coef_rows = coef_rows + (part if j == 0 else pltpu.roll(part, 25 * j, 1))
    coef_pad = jnp.concatenate([coef_rows, jnp.zeros((112, 256), F32)], axis=0).astype(BF)
    answer = dot(own_hot[...], coef_pad).astype(BF)
    for k in range(ny):
        s_c[k] = answer[k * 16:(k + 1) * 16, :]
    r_c[iy] = s_c[iy]
    exch_c("start")

    def total_of(ref, n):
        total = ref[0].astype(F32)
        for k in range(1, n):
            total = total + ref[k].astype(F32)
        return total

    exch_g1("recv")
    sum_y1[iy] = total_of(gw_recv1, nx).astype(BF)
    exch_u1("start")
    exch_g2("recv")
    sum_y2[iy] = total_of(gw_recv2, nx).astype(BF)
    exch_u2("start")

    exch_c("recv")
    rows = dot(back, r_c[...].reshape(256, 256)).astype(BF)
    for k in range(nx):
        s_d[k] = rows[k * 32:(k + 1) * 32, :]
    r_d[ix] = s_d[ix]
    exch_d("start")

    for c in range(len(CHUNKS)):
        for copy in y_copies(c):
            copy.wait_send()
    exch_c("send")
    exch_g1("send")
    exch_g2("send")

    exch_u1("recv")
    out_recv1[ix] = total_of(sum_y1, ny).astype(BF)
    exch_o1("start")
    exch_u2("recv")
    out_recv2[ix] = total_of(sum_y2, ny).astype(BF)
    exch_o2("start")

    exch_d("recv")
    fetched = dot(pick_p[...], r_d[...].reshape(256, 256)).astype(BF)
    keep = jnp.where(iota((16, 256), 0) % 4 == iota((16, 256), 1) // 64, 1.0, 0.0)
    for q in range(8):
        rows16 = fetched[q * 16:(q + 1) * 16, 0:200]
        for r in range(4):
            t = q * 4 + r
            out = dot(rows16, basis[t])
            wanted = keep * jnp.where(iota((16, 256), 0) // 4 == r, 1.0, 0.0)
            dens[t:t + 1, :] = jnp.sum(out * wanted, axis=0, keepdims=True)
    folded = dens[:, 0:128] + dens[:, 128:256]
    tmp256[0:32, :] = folded + pltpu.roll(folded, 64, 1)
    even = tmp256[pl.ds(0, 16, stride=2), :]
    odd_rows = tmp256[pl.ds(1, 16, stride=2), :]
    dens_out[...] = jnp.where(iota((16, 128), 1) < 64, even, odd_rows)

    exch_d("send")
    exch_u1("send")
    exch_u2("send")
    exch_o1("recv")
    exch_o2("recv")
    exch_o1("send")
    exch_o2("send")


def spread_kernel(low, high, dens, dens_out, gw_out):
    dens_out[...] = dens[...]
    for ref, degrees in ((low, (0, 1)), (high, (2, 4, 3))):
        for at, l in enumerate(degrees):
            for k in range(ref.shape[0]):
                gw_out[l, k * 16:(k + 1) * 16, :] = ref[k, at * 16:(at + 1) * 16, :].astype(F32)


def body(nx, ny, irreps, mix_weight, readout, ghost_x, ghost_y, edge_source_row, edge_dst, radial,
         tile_peer, tile_block, tile_count, basis, density_cot):
    irr = jnp.transpose(irreps[0, 0], (1, 0, 2))
    nch = len(CHUNKS)
    dma = pltpu.SemaphoreType.DMA
    vm = pltpu.VMEM
    dens, low, high = pl.pallas_call(
        functools.partial(kernel, nx, ny),
        out_shape=(
            pltpu.VMEM((16, 128), F32),
            pltpu.VMEM((nx, 32, 128), BF),
            pltpu.VMEM((nx, 48, 128), BF),
        ),
        in_specs=[pl.BlockSpec(memory_space=pltpu.HBM)] * 13,
        out_specs=(pl.BlockSpec(memory_space=pltpu.VMEM),) * 3,
        scratch_shapes=[
            vm((5, 128, 128), BF),
            vm((25, 128), BF),
            vm((2, 64), jnp.int32), vm((2, 64), jnp.int32),
            vm((16, 128), jnp.int32), vm((16, 128), jnp.int32),
            vm((25, 1, 2048), F32),
            vm((4, 32), jnp.int32), vm((4, 32), jnp.int32), vm((1, 32), jnp.int32),
            vm((32, 200, 256), BF),
            vm((1, 2048), BF),
            vm((25, 384, 128), BF),
            vm((3200, 128), BF),
            vm((25, 128, 128), BF),
            vm((25, 128, 128), BF),
            vm((128, 128), BF),
            vm((128, 256), BF),
            vm((2048, 384), BF),
            vm((128, 2048), BF),
            vm((640, 2048), BF),
            vm((25, 128, 384), BF),
            vm((25, 128, 128), BF),
            vm((25, 128, 128), F32),
            vm((25, 128, 128), BF),
            vm((128, 128), F32),
            vm((128, 128), F32),
            vm((128, 128), F32),
            vm((128, 128), F32),
            vm((256, 128), F32),
            vm((nx, 32, 256), BF), vm((nx, 32, 256), BF),
            vm((ny, 16, 256), BF), vm((ny, 16, 256), BF),
            vm((ny, 16, 256), BF), vm((ny, 16, 256), BF),
            vm((nx, 32, 256), BF), vm((nx, 32, 256), BF),
            vm((128, 256), BF),
            vm((256, 128), BF),
            vm((32, 256), F32),
            vm((nx, 48, 128), BF), vm((nx, 48, 128), BF),
            vm((nx, 32, 128), BF), vm((nx, 32, 128), BF),
            vm((ny, 48, 128), BF), vm((ny, 32, 128), BF),
            dma((13,)),
            dma((nch, 2)), dma((nch, 2)), dma((nch, 2)), dma((nch, 2)),
            dma((1,)), dma((1,)), dma((1,)), dma((1,)), dma((1,)), dma((1,)), dma((1,)), dma((1,)),
            dma((2,)), dma((2,)), dma((2,)), dma((2,)), dma((2,)), dma((2,)),
        ],
        compiler_params=pltpu.CompilerParams(
            collective_id=0, has_side_effects=True, vmem_limit_bytes=60 * 1024 * 1024
        ),
    )(
        irr,
        mix_weight,
        readout,
        ghost_x.reshape(2, 64),
        ghost_y.reshape(2, 64),
        edge_source_row.reshape(16, 128),
        edge_dst.reshape(16, 128),
        radial.reshape(25, 1, 2048),
        jnp.transpose(tile_peer[0, 0]),
        jnp.transpose(tile_block[0, 0]),
        tile_count.reshape(1, 32),
        basis.reshape(32, 200, 256),
        density_cot.reshape(1, 2048),
    )
    dens, gw = pl.pallas_call(
        spread_kernel,
        out_shape=(
            jax.ShapeDtypeStruct((16, 128), F32),
            jax.ShapeDtypeStruct((5, 128, 128), F32),
        ),
        compiler_params=pltpu.CompilerParams(vmem_limit_bytes=4 * 1024 * 1024),
    )(low, high, dens)
    return dens.reshape(1, 1, 2048), gw


def solution(mesh):
    nx, ny = mesh.shape["gx"], mesh.shape["gy"]
    placed = (
        P("gx", "gy", None, None, None),
        P(),
        P(),
        P("gx", "gy", None, None),
        P("gx", "gy", None, None),
        P("gx", "gy", None),
        P("gx", "gy", None),
        P("gx", "gy", None, None),
        P("gx", "gy", None, None),
        P("gx", "gy", None, None),
        P("gx", "gy", None),
        P("gx", "gy", None, None, None),
        P("gx", "gy", None),
    )
    return jax.shard_map(
        functools.partial(body, nx, ny),
        mesh=mesh, in_specs=placed, out_specs=(P("gx", "gy", None), P()), check_vma=False,
    )
```

```python
import functools

import jax
import jax.numpy as jnp
from jax import lax
from jax.experimental import pallas as pl
from jax.experimental.pallas import tpu as pltpu
from jax.sharding import PartitionSpec as P

MESH = pl.DeviceIdType.MESH
BF = jnp.bfloat16
F32 = jnp.float32

CHUNKS = ((0, 1), (4, 6), (6, 9), (16, 20), (20, 25), (9, 13), (13, 16), (1, 4))
DEGREES = 5


def degree_of(m):
    l = 0
    while (l + 1) * (l + 1) <= m:
        l += 1
    return l


def iota(shape, dim):
    return lax.broadcasted_iota(jnp.int32, shape, dim)


def dot(a, b):
    return jnp.dot(a, b, preferred_element_type=F32)


def dot_nt(a, b):
    return lax.dot_general(a, b, (((1,), (1,)), ((), ())), preferred_element_type=F32)


def dot_tn(a, b):
    return lax.dot_general(a, b, (((0,), (0,)), ((), ())), preferred_element_type=F32)


def kernel(
    nx, ny,
    irr_h, w_h, ro_h, gx_h, gy_h, src_h, dst_h, rad_h, peer_h, block_h, count_h, basis_h, cot_h,
    dens_out, out_recv2, out_recv1,
    w, ro, gxi, gyi, src, dst, rad, peer, block, count, basis, cot, table, roc, xface, yface, hot_x, hot_y, source_hot, dst_mask, scaled, op,
    y_st, g_st, gg_st, gate, coef, gate_grad, atom_grad, tmp256,
    s_a, r_a, s_b, r_b, s_c, r_c, s_d, r_d, pick_p, own_hot, dens,
    gw_send1, gw_recv1, gw_send2, gw_recv2, sum_y1, sum_y2,
    in_sem, xs_sem, xr_sem, ys_sem, yr_sem,
    as_sem, ar_sem, bs_sem, br_sem, cs_sem, cr_sem, ds_sem, dr_sem,
    ws_sem, wr_sem, us_sem, ur_sem, os_sem, or_sem,
):
    ix = lax.axis_index("gx")
    iy = lax.axis_index("gy")
    left, right = (ix + nx - 1) % nx, (ix + 1) % nx
    lower, upper = (iy + ny - 1) % ny, (iy + 1) % ny

    barrier = pltpu.get_barrier_semaphore()

    def hops(d):
        return min(d, 4 - d)

    z_now, core_now, y_now, x_now = ix // 2, ix % 2, iy // 4, iy % 4
    x_steps = sorted(((dz, dc) for dz in range(4) for dc in range(2)), key=lambda v: -(2 * hops(v[0]) + v[1]))
    y_steps = sorted(((dy, dx) for dy in range(4) for dx in range(4)), key=lambda v: -(hops(v[0]) + hops(v[1])))
    others_x = [(z_now + dz) % 4 * 2 + (core_now + dc) % 2 for dz, dc in x_steps if dz or dc]
    others_y = [(y_now + dy) % 4 * 4 + (x_now + dx) % 4 for dy, dx in y_steps if dy or dx]
    for other in others_y:
        pl.semaphore_signal(barrier, inc=1, device_id=(ix, other), device_id_type=MESH)
    for other in others_x:
        pl.semaphore_signal(barrier, inc=1, device_id=(other, iy), device_id_type=MESH)

    local = {}
    for n, (name, held, here) in enumerate((
        ("gxi", gx_h, gxi), ("irr", irr_h, table.at[:, pl.ds(0, 128), :]), ("gyi", gy_h, gyi), ("src", src_h, src), ("dst", dst_h, dst),
        ("rad", rad_h, rad), ("peer", peer_h, peer), ("block", block_h, block), ("count", count_h, count),
        ("cot", cot_h, cot), ("basis", basis_h, basis), ("w", w_h, w), ("ro", ro_h, ro),
    )):
        local[name] = pltpu.make_async_copy(held, here, in_sem.at[n])
        local[name].start()

    def arrive(*names):
        for name in names:
            local[name].wait()

    def remote(s, d, ssem, rsem, i, j):
        return pltpu.make_async_remote_copy(
            src_ref=s, dst_ref=d, send_sem=ssem, recv_sem=rsem, device_id=(i, j), device_id_type=MESH
        )

    def x_copies(c):
        lo, hi = CHUNKS[c]
        n = hi - lo
        return (
            remote(xface.at[pl.ds(lo, n), pl.ds(64, 64), :], table.at[pl.ds(lo, n), pl.ds(128, 64), :],
                   xs_sem.at[c, 0], xr_sem.at[c, 0], right, iy),
            remote(xface.at[pl.ds(lo, n), pl.ds(0, 64), :], table.at[pl.ds(lo, n), pl.ds(192, 64), :],
                   xs_sem.at[c, 1], xr_sem.at[c, 1], left, iy),
        )

    def y_copies(c):
        lo, hi = CHUNKS[c]
        n = hi - lo
        return (
            remote(yface.at[pl.ds(lo, n), pl.ds(64, 64), :], table.at[pl.ds(lo, n), pl.ds(256, 64), :],
                   ys_sem.at[c, 0], yr_sem.at[c, 0], ix, upper),
            remote(yface.at[pl.ds(lo, n), pl.ds(0, 64), :], table.at[pl.ds(lo, n), pl.ds(320, 64), :],
                   ys_sem.at[c, 1], yr_sem.at[c, 1], ix, lower),
        )

    def ghost_row(ref):
        return jnp.concatenate([ref[0:1, :], ref[1:2, :]], axis=1)

    arrive("gxi")
    hot_x[...] = jnp.where(iota((128, 128), 0) == ghost_row(gxi), 1.0, 0.0).T.astype(BF)
    arrive("irr")

    chooser = hot_x[...]
    for lo, hi in CHUNKS:
        for m in range(lo, hi):
            xface[m] = dot(chooser, table[m, 0:128, :]).astype(BF)

    arrive("gyi")
    gy_row = ghost_row(gyi)
    for half in range(2):
        hot_y[:, half * 128:(half + 1) * 128] = (
            jnp.where(iota((128, 128), 0) + half * 128 == gy_row, 1.0, 0.0).T.astype(BF)
        )

    def send_y(c):
        for copy in x_copies(c):
            copy.wait_recv()
        lo, hi = CHUNKS[c]
        for m in range(lo, hi):
            yface[m] = dot(hot_y[...], table[m, 0:256, :]).astype(BF)
        for copy in y_copies(c):
            copy.start()

    def build_op(c):
        lo, hi = CHUNKS[c]
        n = hi - lo
        for i in range(n):
            row = rad[lo + i].astype(BF)
            scaled[i * 128:(i + 1) * 128, :] = dst_mask[...] * jnp.broadcast_to(row, (128, 2048))
        built = dot(scaled[0:n * 128, :], source_hot[...])
        for i in range(n):
            op[lo + i] = built[i * 128:(i + 1) * 128, :].astype(BF)

    arrive("peer", "block", "count", "cot")

    def slot_row(ref):
        return jnp.concatenate([ref[k:k + 1, :] for k in range(4)], axis=1)

    peer_row = slot_row(peer)
    same = (jnp.broadcast_to(peer_row, (128, 128)).astype(F32).T == peer_row.astype(F32)) & (
        iota((128, 128), 0) < iota((128, 128), 1)
    )
    rank = jnp.sum(jnp.where(same, 1.0, 0.0), axis=0, keepdims=True).astype(jnp.int32)
    live_row = (iota((1, 128), 1) // 32) < jnp.concatenate([count[...]] * 4, axis=1)
    position = jnp.where(live_row, peer_row * 2 + rank, -1)
    chosen = jnp.where(iota((256, 128), 0) == position, 1.0, 0.0)
    slot_n = iota((128, 128), 0)
    reorder = jnp.where(iota((128, 128), 1) == slot_n % 4 * 32 + slot_n // 4, 1.0, 0.0).astype(BF)
    for half in range(2):
        pick_p[:, half * 128:(half + 1) * 128] = dot_nt(
            reorder, chosen[half * 128:(half + 1) * 128, :].astype(BF)
        ).astype(BF)
    cot_f = cot[...].astype(F32)
    cot_rows = jnp.concatenate([cot_f[:, u * 128:(u + 1) * 128] for u in range(16)], axis=0).astype(BF)
    tile_n = slot_n % 32
    spread = jnp.where(iota((128, 16), 1) == iota((128, 16), 0) % 32 // 2, 1.0, 0.0).astype(BF)
    picked = dot(spread, cot_rows)
    mine = jnp.where((iota((128, 128), 1) // 64) == tile_n % 2, picked, pltpu.roll(picked, 64, 1))
    both = jnp.concatenate([mine, mine], axis=1)
    weights = jnp.where(iota((128, 256), 1) // 64 == iota((128, 256), 0) // 32, both, 0.0)

    weights_t = jnp.concatenate([weights[:, 0:128].T, weights[:, 128:256].T], axis=0).astype(BF)
    arrive("basis")

    lane_tile = iota((200, 128), 1) % 32

    slot_grad = jnp.zeros((200, 128), F32)
    for t in range(32):
        slot_grad = jnp.where(lane_tile == t, dot(basis[t], weights_t), slot_grad)
    id_rows = jnp.where(iota((56, 128), 0) == 0, jnp.broadcast_to(slot_row(block).astype(F32), (56, 128)), 0.0)
    tmp256[...] = jnp.concatenate([slot_grad, id_rows], axis=0)
    sent = dot_nt(chosen.astype(BF), tmp256[...].astype(BF)).astype(BF)
    for k in range(nx):
        s_a[k] = sent[k * 32:(k + 1) * 32, :]
    r_a[ix] = s_a[ix]

    def exchange(axis, n, s, r, ssem, rsem, mode):
        me = ix if axis == "x" else iy
        if mode != "start":
            to = (right, iy) if axis == "x" else (ix, upper)
            everything = remote(r.at[pl.ds(0, n - 1)], r.at[pl.ds(0, n - 1)], ssem, rsem, *to)
            everything.wait_recv() if mode == "recv" else everything.wait_send()
            return
        for other in others_x if axis == "x" else others_y:
            to = (other, iy) if axis == "x" else (ix, other)
            remote(s(other), r.at[me], ssem, rsem, *to).start()

    def slot_of(ref):
        return lambda k: ref.at[k]

    exch_a = functools.partial(exchange, "x", nx, slot_of(s_a), r_a, as_sem.at[0], ar_sem.at[0])
    exch_b = functools.partial(exchange, "y", ny, slot_of(s_b), r_b, bs_sem.at[0], br_sem.at[0])
    exch_c = functools.partial(exchange, "y", ny, slot_of(s_c), r_c, cs_sem.at[0], cr_sem.at[0])
    exch_d = functools.partial(exchange, "x", nx, slot_of(s_d), r_d, ds_sem.at[0], dr_sem.at[0])
    exch_g1 = functools.partial(exchange, "x", nx, slot_of(gw_send1), gw_recv1, ws_sem.at[0], wr_sem.at[0])
    exch_g2 = functools.partial(exchange, "x", nx, slot_of(gw_send2), gw_recv2, ws_sem.at[1], wr_sem.at[1])
    exch_u1 = functools.partial(exchange, "y", ny, lambda k: sum_y1.at[iy], sum_y1, us_sem.at[0], ur_sem.at[0])
    exch_u2 = functools.partial(exchange, "y", ny, lambda k: sum_y2.at[iy], sum_y2, us_sem.at[1], ur_sem.at[1])
    exch_o1 = functools.partial(exchange, "x", nx, lambda k: out_recv1.at[ix], out_recv1, os_sem.at[0], or_sem.at[0])
    exch_o2 = functools.partial(exchange, "x", nx, lambda k: out_recv2.at[ix], out_recv2, os_sem.at[1], or_sem.at[1])

    pl.semaphore_wait(barrier, nx + ny - 2)
    exch_a("start")
    for c in range(len(CHUNKS)):
        for copy in x_copies(c):
            copy.start()

    arrive("src", "dst", "rad")
    src_cols = jnp.concatenate([src[...].astype(F32), jnp.zeros((112, 128), F32)], axis=0).T
    lane384 = iota((128, 384), 1).astype(F32)
    sub128 = iota((128, 128), 0)
    for k in range(16):
        source_hot[k * 128:(k + 1) * 128, :] = jnp.where(src_cols[:, k:k + 1] == lane384, 1.0, 0.0).astype(BF)
        dst_mask[:, k * 128:(k + 1) * 128] = jnp.where(sub128 == dst[k:k + 1, :], 1.0, 0.0).astype(BF)

    build_op(0)
    build_op(1)
    build_op(2)
    build_op(3)
    send_y(0)
    send_y(1)
    send_y(2)
    n_i, n_j = iota((256, 256), 0), iota((256, 256), 1)
    turned = (n_i % 16) // 2 * 32 + n_i // 16 * 2 + n_i % 2
    turn = jnp.where(n_j == turned, 1.0, 0.0).astype(BF)
    back = jnp.where(n_j == n_i % 32 // 2 * 16 + n_i // 32 * 2 + n_i % 2, 1.0, 0.0).astype(BF)
    exch_a("recv")
    rows = dot(turn, r_a[...].reshape(256, 256)).astype(BF)
    for k in range(ny):
        s_b[k] = rows[k * 16:(k + 1) * 16, :]
    r_b[iy] = s_b[iy]
    exch_b("start")

    build_op(4)
    send_y(3)
    send_y(4)

    send_y(5)
    send_y(6)
    send_y(7)

    build_op(5)
    build_op(6)
    build_op(7)

    arrive("w", "ro")
    ro_f = ro[...].astype(F32)
    ro_cols = jnp.concatenate([ro_f, jnp.zeros((103, 128), F32)], axis=0).T
    lane128 = iota((128, 128), 1)
    coef[...] = jnp.zeros((128, 128), F32)
    for m in range(25):
        roc[m * 128:(m + 1) * 128, :] = jnp.where(lane128 == m, ro_cols, 0.0).astype(BF)

    def forward(c):
        for copy in y_copies(c):
            copy.wait_recv()
        lo, hi = CHUNKS[c]
        ys = [dot(op[m], table[m]).astype(BF) for m in range(lo, hi)]
        gs = [dot(y, w[degree_of(lo + i)]) for i, y in enumerate(ys)]
        if lo == 0:
            gate[...] = jax.nn.sigmoid(gs[0])
        for i, (y, g) in enumerate(zip(ys, gs)):
            y_st[lo + i] = y
            g_st[lo + i] = g
        if c + 1 < len(CHUNKS):
            coefficients(c, gs)

    def coefficients(c, gs):
        lo, hi = CHUNKS[c]
        s = gate[...]
        updated = [(table[lo + i, 0:128, :].astype(F32) + s * g).astype(BF) for i, g in enumerate(gs)]
        wide = updated[0] if len(updated) == 1 else jnp.concatenate(updated, axis=1)
        coef[...] += dot(wide, roc[lo * 128:hi * 128, :])

    def backward(c):
        lo, hi = CHUNKS[c]
        total = gate_grad[...]
        ag = atom_grad[...]
        for m in range(lo, hi):
            gu = ag[:, m:m + 1] * ro_f[m:m + 1, :]
            total = total + gu * g_st[m]
            if m > 0:
                gg_st[m] = (gu * gate[...]).astype(BF)
        gate_grad[...] = total

    def weight_grad(l, held, at):
        lo, hi = l * l, (l + 1) * (l + 1)
        n = (hi - lo) * 128
        part = dot_tn(y_st[lo:hi].reshape(n, 128), gg_st[lo:hi].reshape(n, 128)).astype(BF)
        for k in range(nx):
            held[k, at * 16:(at + 1) * 16, :] = part[k * 16:(k + 1) * 16, :]

    forward(0)
    forward(1)
    forward(2)
    forward(3)
    forward(4)

    exch_b("recv")
    incoming = r_b[...].reshape(256, 256)
    ids = incoming[:, 128:256].astype(F32)[:, 72:73]
    owner = jnp.where(ids == iota((256, 128), 1).astype(F32), 1.0, 0.0)
    own_hot[...] = owner.astype(BF)
    owner_t = jnp.concatenate([owner[0:128, :].T[0:16, :], owner[128:256, :].T[0:16, :]], axis=1).astype(BF)
    block_grad = dot(owner_t, incoming)
    for j in range(8):
        moved = block_grad if j == 0 else pltpu.roll(block_grad, 256 - 25 * j, 1)
        atom_grad[pl.ds(j, 16, stride=8), :] = moved[:, 0:128]
    gate_grad[...] = jnp.zeros((128, 128), F32)

    for c in range(5):
        backward(c)
    weight_grad(2, gw_send1, 0)
    weight_grad(4, gw_send1, 1)
    forward(5)
    backward(5)
    exch_a("send")
    exch_b("send")
    for c in range(len(CHUNKS)):
        for copy in x_copies(c):
            copy.wait_send()
    forward(6)
    backward(6)
    weight_grad(3, gw_send1, 2)
    gw_recv1[ix] = gw_send1[ix]
    exch_g1("start")
    forward(7)
    backward(7)
    weight_grad(1, gw_send2, 1)
    gu = atom_grad[:, 0:1] * ro_f[0:1, :]
    s = gate[...]
    gg_st[0] = (gu * s + gate_grad[...] * s * (1.0 - s)).astype(BF)
    weight_grad(0, gw_send2, 0)
    gw_recv2[ix] = gw_send2[ix]
    exch_g2("start")

    coefficients(7, [g_st[m] for m in range(*CHUNKS[7])])
    coef_rows = jnp.zeros((16, 256), F32)
    valid = jnp.where(iota((16, 256), 1) < 25, 1.0, 0.0)
    for j in range(8):
        part = jnp.concatenate([coef[pl.ds(j, 16, stride=8), :], jnp.zeros((16, 128), F32)], axis=1) * valid
        coef_rows = coef_rows + (part if j == 0 else pltpu.roll(part, 25 * j, 1))
    coef_pad = jnp.concatenate([coef_rows, jnp.zeros((112, 256), F32)], axis=0).astype(BF)
    answer = dot(own_hot[...], coef_pad).astype(BF)
    for k in range(ny):
        s_c[k] = answer[k * 16:(k + 1) * 16, :]
    r_c[iy] = s_c[iy]
    exch_c("start")

    def total_of(ref, n):
        total = ref[0].astype(F32)
        for k in range(1, n):
            total = total + ref[k].astype(F32)
        return total

    exch_g1("recv")
    sum_y1[iy] = total_of(gw_recv1, nx).astype(BF)
    exch_u1("start")
    exch_g2("recv")
    sum_y2[iy] = total_of(gw_recv2, nx).astype(BF)
    exch_u2("start")

    exch_c("recv")
    rows = dot(back, r_c[...].reshape(256, 256)).astype(BF)
    for k in range(nx):
        s_d[k] = rows[k * 32:(k + 1) * 32, :]
    r_d[ix] = s_d[ix]
    exch_d("start")

    for c in range(len(CHUNKS)):
        for copy in y_copies(c):
            copy.wait_send()
    exch_c("send")
    exch_g1("send")
    exch_g2("send")

    exch_u1("recv")
    out_recv1[ix] = total_of(sum_y1, ny).astype(BF)
    exch_o1("start")
    exch_u2("recv")
    out_recv2[ix] = total_of(sum_y2, ny).astype(BF)
    exch_o2("start")

    exch_d("recv")
    fetched = dot(pick_p[...], r_d[...].reshape(256, 256)).astype(BF)
    keep = jnp.where(iota((16, 256), 0) % 4 == iota((16, 256), 1) // 64, 1.0, 0.0)
    for q in range(8):
        rows16 = fetched[q * 16:(q + 1) * 16, 0:200]
        for r in range(4):
            t = q * 4 + r
            out = dot(rows16, basis[t])
            wanted = keep * jnp.where(iota((16, 256), 0) // 4 == r, 1.0, 0.0)
            dens[t:t + 1, :] = jnp.sum(out * wanted, axis=0, keepdims=True)
    folded = dens[:, 0:128] + dens[:, 128:256]
    tmp256[0:32, :] = folded + pltpu.roll(folded, 64, 1)
    even = tmp256[pl.ds(0, 16, stride=2), :]
    odd_rows = tmp256[pl.ds(1, 16, stride=2), :]
    dens_out[...] = jnp.where(iota((16, 128), 1) < 64, even, odd_rows)

    exch_d("send")
    exch_u1("send")
    exch_u2("send")
    exch_o1("recv")
    exch_o2("recv")
    exch_o1("send")
    exch_o2("send")


def spread_kernel(low, high, dens, dens_out, gw_out):
    dens_out[...] = dens[...]
    for ref, degrees in ((low, (0, 1)), (high, (2, 4, 3))):
        for at, l in enumerate(degrees):
            for k in range(ref.shape[0]):
                gw_out[l, k * 16:(k + 1) * 16, :] = ref[k, at * 16:(at + 1) * 16, :].astype(F32)


def body(nx, ny, irreps, mix_weight, readout, ghost_x, ghost_y, edge_source_row, edge_dst, radial,
         tile_peer, tile_block, tile_count, basis, density_cot):
    irr = jnp.transpose(irreps[0, 0], (1, 0, 2))
    nch = len(CHUNKS)
    dma = pltpu.SemaphoreType.DMA
    vm = pltpu.VMEM
    dens, low, high = pl.pallas_call(
        functools.partial(kernel, nx, ny),
        out_shape=(
            pltpu.VMEM((16, 128), F32),
            pltpu.VMEM((nx, 32, 128), BF),
            pltpu.VMEM((nx, 48, 128), BF),
        ),
        in_specs=[pl.BlockSpec(memory_space=pltpu.HBM)] * 13,
        out_specs=(pl.BlockSpec(memory_space=pltpu.VMEM),) * 3,
        scratch_shapes=[
            vm((5, 128, 128), BF),
            vm((25, 128), BF),
            vm((2, 64), jnp.int32), vm((2, 64), jnp.int32),
            vm((16, 128), jnp.int32), vm((16, 128), jnp.int32),
            vm((25, 1, 2048), F32),
            vm((4, 32), jnp.int32), vm((4, 32), jnp.int32), vm((1, 32), jnp.int32),
            vm((32, 200, 256), BF),
            vm((1, 2048), BF),
            vm((25, 384, 128), BF),
            vm((3200, 128), BF),
            vm((25, 128, 128), BF),
            vm((25, 128, 128), BF),
            vm((128, 128), BF),
            vm((128, 256), BF),
            vm((2048, 384), BF),
            vm((128, 2048), BF),
            vm((640, 2048), BF),
            vm((25, 128, 384), BF),
            vm((25, 128, 128), BF),
            vm((25, 128, 128), F32),
            vm((25, 128, 128), BF),
            vm((128, 128), F32),
            vm((128, 128), F32),
            vm((128, 128), F32),
            vm((128, 128), F32),
            vm((256, 128), F32),
            vm((nx, 32, 256), BF), vm((nx, 32, 256), BF),
            vm((ny, 16, 256), BF), vm((ny, 16, 256), BF),
            vm((ny, 16, 256), BF), vm((ny, 16, 256), BF),
            vm((nx, 32, 256), BF), vm((nx, 32, 256), BF),
            vm((128, 256), BF),
            vm((256, 128), BF),
            vm((32, 256), F32),
            vm((nx, 48, 128), BF), vm((nx, 48, 128), BF),
            vm((nx, 32, 128), BF), vm((nx, 32, 128), BF),
            vm((ny, 48, 128), BF), vm((ny, 32, 128), BF),
            dma((13,)),
            dma((nch, 2)), dma((nch, 2)), dma((nch, 2)), dma((nch, 2)),
            dma((1,)), dma((1,)), dma((1,)), dma((1,)), dma((1,)), dma((1,)), dma((1,)), dma((1,)),
            dma((2,)), dma((2,)), dma((2,)), dma((2,)), dma((2,)), dma((2,)),
        ],
        compiler_params=pltpu.CompilerParams(
            collective_id=0, has_side_effects=True, vmem_limit_bytes=60 * 1024 * 1024
        ),
    )(
        irr,
        mix_weight,
        readout,
        ghost_x.reshape(2, 64),
        ghost_y.reshape(2, 64),
        edge_source_row.reshape(16, 128),
        edge_dst.reshape(16, 128),
        radial.reshape(25, 1, 2048),
        jnp.transpose(tile_peer[0, 0]),
        jnp.transpose(tile_block[0, 0]),
        tile_count.reshape(1, 32),
        basis.reshape(32, 200, 256),
        density_cot.reshape(1, 2048),
    )
    dens, gw = pl.pallas_call(
        spread_kernel,
        out_shape=(
            jax.ShapeDtypeStruct((16, 128), F32),
            jax.ShapeDtypeStruct((5, 128, 128), F32),
        ),
        compiler_params=pltpu.CompilerParams(vmem_limit_bytes=4 * 1024 * 1024),
    )(low, high, dens)
    return dens.reshape(1, 1, 2048), gw


def solution(mesh):
    nx, ny = mesh.shape["gx"], mesh.shape["gy"]
    placed = (
        P("gx", "gy", None, None, None),
        P(),
        P(),
        P("gx", "gy", None, None),
        P("gx", "gy", None, None),
        P("gx", "gy", None),
        P("gx", "gy", None),
        P("gx", "gy", None, None),
        P("gx", "gy", None, None),
        P("gx", "gy", None, None),
        P("gx", "gy", None),
        P("gx", "gy", None, None, None),
        P("gx", "gy", None),
    )
    return jax.shard_map(
        functools.partial(body, nx, ny),
        mesh=mesh, in_specs=placed, out_specs=(P("gx", "gy", None), P()), check_vma=False,
    )
```

```python
import functools

import jax
import jax.numpy as jnp
from jax import lax
from jax.experimental import pallas as pl
from jax.experimental.pallas import tpu as pltpu
from jax.sharding import PartitionSpec as P

MESH = pl.DeviceIdType.MESH
BF = jnp.bfloat16
F32 = jnp.float32

CHUNKS = ((0, 1), (4, 6), (6, 9), (16, 20), (20, 25), (9, 13), (13, 16), (1, 4))
DEGREES = 5


def degree_of(m):
    l = 0
    while (l + 1) * (l + 1) <= m:
        l += 1
    return l


def iota(shape, dim):
    return lax.broadcasted_iota(jnp.int32, shape, dim)


def dot(a, b):
    return jnp.dot(a, b, preferred_element_type=F32)


def dot_nt(a, b):
    return lax.dot_general(a, b, (((1,), (1,)), ((), ())), preferred_element_type=F32)


def dot_tn(a, b):
    return lax.dot_general(a, b, (((0,), (0,)), ((), ())), preferred_element_type=F32)


def kernel(
    nx, ny,
    irr_h, w_h, ro_h, gx_h, gy_h, src_h, dst_h, rad_h, peer_h, block_h, count_h, basis_h, cot_h,
    dens_out, out_recv2, out_recv1,
    w, ro, gxi, gyi, src, dst, rad, peer, block, count, basis, cot, table, roc, xface, yface, hot_x, hot_y, source_hot, dst_mask, scaled, op,
    y_st, g_st, gg_st, gate, coef, gate_grad, atom_grad, tmp256,
    s_a, r_a, s_b, r_b, s_c, r_c, s_d, r_d, pick_p, own_hot, dens,
    gw_send1, gw_recv1, gw_send2, gw_recv2, sum_y1, sum_y2,
    in_sem, xs_sem, xr_sem, ys_sem, yr_sem,
    as_sem, ar_sem, bs_sem, br_sem, cs_sem, cr_sem, ds_sem, dr_sem,
    ws_sem, wr_sem, us_sem, ur_sem, os_sem, or_sem,
):
    ix = lax.axis_index("gx")
    iy = lax.axis_index("gy")
    left, right = (ix + nx - 1) % nx, (ix + 1) % nx
    lower, upper = (iy + ny - 1) % ny, (iy + 1) % ny

    local = {}
    for n, (name, held, here) in enumerate((
        ("gxi", gx_h, gxi), ("irr", irr_h, table.at[:, pl.ds(0, 128), :]), ("gyi", gy_h, gyi), ("src", src_h, src), ("dst", dst_h, dst),
        ("rad", rad_h, rad), ("peer", peer_h, peer), ("block", block_h, block), ("count", count_h, count),
        ("cot", cot_h, cot), ("basis", basis_h, basis), ("w", w_h, w), ("ro", ro_h, ro),
    )):
        local[name] = pltpu.make_async_copy(held, here, in_sem.at[n])
        local[name].start()

    barrier = pltpu.get_barrier_semaphore()

    def hops(d):
        return min(d, 4 - d)

    z_now, core_now, y_now, x_now = ix // 2, ix % 2, iy // 4, iy % 4
    x_steps = sorted(((dz, dc) for dz in range(4) for dc in range(2)), key=lambda v: -(2 * hops(v[0]) + v[1]))
    y_steps = sorted(((dy, dx) for dy in range(4) for dx in range(4)), key=lambda v: -(hops(v[0]) + hops(v[1])))
    others_x = [(z_now + dz) % 4 * 2 + (core_now + dc) % 2 for dz, dc in x_steps if dz or dc]
    others_y = [(y_now + dy) % 4 * 4 + (x_now + dx) % 4 for dy, dx in y_steps if dy or dx]
    for other in others_y:
        pl.semaphore_signal(barrier, inc=1, device_id=(ix, other), device_id_type=MESH)
    for other in others_x:
        pl.semaphore_signal(barrier, inc=1, device_id=(other, iy), device_id_type=MESH)

    def arrive(*names):
        for name in names:
            local[name].wait()

    def remote(s, d, ssem, rsem, i, j):
        return pltpu.make_async_remote_copy(
            src_ref=s, dst_ref=d, send_sem=ssem, recv_sem=rsem, device_id=(i, j), device_id_type=MESH
        )

    def x_copies(c):
        lo, hi = CHUNKS[c]
        n = hi - lo
        return (
            remote(xface.at[pl.ds(lo, n), pl.ds(64, 64), :], table.at[pl.ds(lo, n), pl.ds(128, 64), :],
                   xs_sem.at[c, 0], xr_sem.at[c, 0], right, iy),
            remote(xface.at[pl.ds(lo, n), pl.ds(0, 64), :], table.at[pl.ds(lo, n), pl.ds(192, 64), :],
                   xs_sem.at[c, 1], xr_sem.at[c, 1], left, iy),
        )

    def y_copies(c):
        lo, hi = CHUNKS[c]
        n = hi - lo
        return (
            remote(yface.at[pl.ds(lo, n), pl.ds(64, 64), :], table.at[pl.ds(lo, n), pl.ds(256, 64), :],
                   ys_sem.at[c, 0], yr_sem.at[c, 0], ix, upper),
            remote(yface.at[pl.ds(lo, n), pl.ds(0, 64), :], table.at[pl.ds(lo, n), pl.ds(320, 64), :],
                   ys_sem.at[c, 1], yr_sem.at[c, 1], ix, lower),
        )

    def ghost_row(ref):
        return jnp.concatenate([ref[0:1, :], ref[1:2, :]], axis=1)

    arrive("gxi")
    hot_x[...] = jnp.where(iota((128, 128), 0) == ghost_row(gxi), 1.0, 0.0).T.astype(BF)
    arrive("irr")

    chooser = hot_x[...]
    for lo, hi in CHUNKS:
        for m in range(lo, hi):
            xface[m] = dot(chooser, table[m, 0:128, :]).astype(BF)

    arrive("gyi")
    gy_row = ghost_row(gyi)
    for half in range(2):
        hot_y[:, half * 128:(half + 1) * 128] = (
            jnp.where(iota((128, 128), 0) + half * 128 == gy_row, 1.0, 0.0).T.astype(BF)
        )

    def send_y(c):
        for copy in x_copies(c):
            copy.wait_recv()
        lo, hi = CHUNKS[c]
        for m in range(lo, hi):
            yface[m] = dot(hot_y[...], table[m, 0:256, :]).astype(BF)
        for copy in y_copies(c):
            copy.start()

    def build_op(c):
        lo, hi = CHUNKS[c]
        n = hi - lo
        for i in range(n):
            row = rad[lo + i].astype(BF)
            scaled[i * 128:(i + 1) * 128, :] = dst_mask[...] * jnp.broadcast_to(row, (128, 2048))
        built = dot(scaled[0:n * 128, :], source_hot[...])
        for i in range(n):
            op[lo + i] = built[i * 128:(i + 1) * 128, :].astype(BF)

    arrive("peer", "block", "count", "cot")

    def slot_row(ref):
        return jnp.concatenate([ref[k:k + 1, :] for k in range(4)], axis=1)

    peer_row = slot_row(peer)
    same = (jnp.broadcast_to(peer_row, (128, 128)).astype(F32).T == peer_row.astype(F32)) & (
        iota((128, 128), 0) < iota((128, 128), 1)
    )
    rank = jnp.sum(jnp.where(same, 1.0, 0.0), axis=0, keepdims=True).astype(jnp.int32)
    live_row = (iota((1, 128), 1) // 32) < jnp.concatenate([count[...]] * 4, axis=1)
    position = jnp.where(live_row, peer_row * 2 + rank, -1)
    chosen = jnp.where(iota((256, 128), 0) == position, 1.0, 0.0)
    slot_n = iota((128, 128), 0)
    reorder = jnp.where(iota((128, 128), 1) == slot_n % 4 * 32 + slot_n // 4, 1.0, 0.0).astype(BF)
    for half in range(2):
        pick_p[:, half * 128:(half + 1) * 128] = dot_nt(
            reorder, chosen[half * 128:(half + 1) * 128, :].astype(BF)
        ).astype(BF)
    cot_f = cot[...].astype(F32)
    cot_rows = jnp.concatenate([cot_f[:, u * 128:(u + 1) * 128] for u in range(16)], axis=0).astype(BF)
    tile_n = slot_n % 32
    spread = jnp.where(iota((128, 16), 1) == iota((128, 16), 0) % 32 // 2, 1.0, 0.0).astype(BF)
    picked = dot(spread, cot_rows)
    mine = jnp.where((iota((128, 128), 1) // 64) == tile_n % 2, picked, pltpu.roll(picked, 64, 1))
    both = jnp.concatenate([mine, mine], axis=1)
    weights = jnp.where(iota((128, 256), 1) // 64 == iota((128, 256), 0) // 32, both, 0.0)

    weights_t = jnp.concatenate([weights[:, 0:128].T, weights[:, 128:256].T], axis=0).astype(BF)
    arrive("basis")

    lane_tile = iota((200, 128), 1) % 32

    slot_grad = jnp.zeros((200, 128), F32)
    for t in range(32):
        slot_grad = jnp.where(lane_tile == t, dot(basis[t], weights_t), slot_grad)
    id_rows = jnp.where(iota((56, 128), 0) == 0, jnp.broadcast_to(slot_row(block).astype(F32), (56, 128)), 0.0)
    tmp256[...] = jnp.concatenate([slot_grad, id_rows], axis=0)
    sent = dot_nt(chosen.astype(BF), tmp256[...].astype(BF)).astype(BF)
    for k in range(nx):
        s_a[k] = sent[k * 32:(k + 1) * 32, :]
    r_a[ix] = s_a[ix]

    def exchange(axis, n, s, r, ssem, rsem, mode):
        me = ix if axis == "x" else iy
        if mode != "start":
            to = (right, iy) if axis == "x" else (ix, upper)
            everything = remote(r.at[pl.ds(0, n - 1)], r.at[pl.ds(0, n - 1)], ssem, rsem, *to)
            everything.wait_recv() if mode == "recv" else everything.wait_send()
            return
        for other in others_x if axis == "x" else others_y:
            to = (other, iy) if axis == "x" else (ix, other)
            remote(s(other), r.at[me], ssem, rsem, *to).start()

    def slot_of(ref):
        return lambda k: ref.at[k]

    exch_a = functools.partial(exchange, "x", nx, slot_of(s_a), r_a, as_sem.at[0], ar_sem.at[0])
    exch_b = functools.partial(exchange, "y", ny, slot_of(s_b), r_b, bs_sem.at[0], br_sem.at[0])
    exch_c = functools.partial(exchange, "y", ny, slot_of(s_c), r_c, cs_sem.at[0], cr_sem.at[0])
    exch_d = functools.partial(exchange, "x", nx, slot_of(s_d), r_d, ds_sem.at[0], dr_sem.at[0])
    exch_g1 = functools.partial(exchange, "x", nx, slot_of(gw_send1), gw_recv1, ws_sem.at[0], wr_sem.at[0])
    exch_g2 = functools.partial(exchange, "x", nx, slot_of(gw_send2), gw_recv2, ws_sem.at[1], wr_sem.at[1])
    exch_u1 = functools.partial(exchange, "y", ny, lambda k: sum_y1.at[iy], sum_y1, us_sem.at[0], ur_sem.at[0])
    exch_u2 = functools.partial(exchange, "y", ny, lambda k: sum_y2.at[iy], sum_y2, us_sem.at[1], ur_sem.at[1])
    exch_o1 = functools.partial(exchange, "x", nx, lambda k: out_recv1.at[ix], out_recv1, os_sem.at[0], or_sem.at[0])
    exch_o2 = functools.partial(exchange, "x", nx, lambda k: out_recv2.at[ix], out_recv2, os_sem.at[1], or_sem.at[1])

    pl.semaphore_wait(barrier, nx + ny - 2)
    exch_a("start")
    for c in range(len(CHUNKS)):
        for copy in x_copies(c):
            copy.start()

    arrive("src", "dst", "rad")
    src_cols = jnp.concatenate([src[...].astype(F32), jnp.zeros((112, 128), F32)], axis=0).T
    lane384 = iota((128, 384), 1).astype(F32)
    sub128 = iota((128, 128), 0)
    for k in range(16):
        source_hot[k * 128:(k + 1) * 128, :] = jnp.where(src_cols[:, k:k + 1] == lane384, 1.0, 0.0).astype(BF)
        dst_mask[:, k * 128:(k + 1) * 128] = jnp.where(sub128 == dst[k:k + 1, :], 1.0, 0.0).astype(BF)

    build_op(0)
    build_op(1)
    build_op(2)
    build_op(3)
    send_y(0)
    send_y(1)
    send_y(2)
    n_i, n_j = iota((256, 256), 0), iota((256, 256), 1)
    turned = (n_i % 16) // 2 * 32 + n_i // 16 * 2 + n_i % 2
    turn = jnp.where(n_j == turned, 1.0, 0.0).astype(BF)
    back = jnp.where(n_j == n_i % 32 // 2 * 16 + n_i // 32 * 2 + n_i % 2, 1.0, 0.0).astype(BF)
    exch_a("recv")
    rows = dot(turn, r_a[...].reshape(256, 256)).astype(BF)
    for k in range(ny):
        s_b[k] = rows[k * 16:(k + 1) * 16, :]
    r_b[iy] = s_b[iy]
    exch_b("start")

    build_op(4)
    send_y(3)
    send_y(4)

    send_y(5)
    send_y(6)
    send_y(7)

    build_op(5)
    build_op(6)
    build_op(7)

    arrive("w", "ro")
    ro_f = ro[...].astype(F32)
    ro_cols = jnp.concatenate([ro_f, jnp.zeros((103, 128), F32)], axis=0).T
    lane128 = iota((128, 128), 1)
    coef[...] = jnp.zeros((128, 128), F32)
    for m in range(25):
        roc[m * 128:(m + 1) * 128, :] = jnp.where(lane128 == m, ro_cols, 0.0).astype(BF)

    def forward(c):
        for copy in y_copies(c):
            copy.wait_recv()
        lo, hi = CHUNKS[c]
        ys = [dot(op[m], table[m]).astype(BF) for m in range(lo, hi)]
        gs = [dot(y, w[degree_of(lo + i)]) for i, y in enumerate(ys)]
        if lo == 0:
            gate[...] = jax.nn.sigmoid(gs[0])
        for i, (y, g) in enumerate(zip(ys, gs)):
            y_st[lo + i] = y
            g_st[lo + i] = g
        if c + 1 < len(CHUNKS):
            coefficients(c, gs)

    def coefficients(c, gs):
        lo, hi = CHUNKS[c]
        s = gate[...]
        updated = [(table[lo + i, 0:128, :].astype(F32) + s * g).astype(BF) for i, g in enumerate(gs)]
        wide = updated[0] if len(updated) == 1 else jnp.concatenate(updated, axis=1)
        coef[...] += dot(wide, roc[lo * 128:hi * 128, :])

    def backward(c):
        lo, hi = CHUNKS[c]
        total = gate_grad[...]
        ag = atom_grad[...]
        for m in range(lo, hi):
            gu = ag[:, m:m + 1] * ro_f[m:m + 1, :]
            total = total + gu * g_st[m]
            if m > 0:
                gg_st[m] = (gu * gate[...]).astype(BF)
        gate_grad[...] = total

    def weight_grad(l, held, at):
        lo, hi = l * l, (l + 1) * (l + 1)
        n = (hi - lo) * 128
        part = dot_tn(y_st[lo:hi].reshape(n, 128), gg_st[lo:hi].reshape(n, 128)).astype(BF)
        for k in range(nx):
            held[k, at * 16:(at + 1) * 16, :] = part[k * 16:(k + 1) * 16, :]

    forward(0)
    forward(1)
    forward(2)

    exch_b("recv")
    incoming = r_b[...].reshape(256, 256)
    ids = incoming[:, 128:256].astype(F32)[:, 72:73]
    owner = jnp.where(ids == iota((256, 128), 1).astype(F32), 1.0, 0.0)
    own_hot[...] = owner.astype(BF)
    owner_t = jnp.concatenate([owner[0:128, :].T[0:16, :], owner[128:256, :].T[0:16, :]], axis=1).astype(BF)
    block_grad = dot(owner_t, incoming)
    for j in range(8):
        moved = block_grad if j == 0 else pltpu.roll(block_grad, 256 - 25 * j, 1)
        atom_grad[pl.ds(j, 16, stride=8), :] = moved[:, 0:128]
    gate_grad[...] = jnp.zeros((128, 128), F32)

    for c in range(3):
        backward(c)
    weight_grad(2, gw_send1, 0)
    forward(3)
    backward(3)
    forward(4)
    backward(4)
    weight_grad(4, gw_send1, 1)
    forward(5)
    backward(5)
    exch_a("send")
    exch_b("send")
    for c in range(len(CHUNKS)):
        for copy in x_copies(c):
            copy.wait_send()
    forward(6)
    backward(6)
    weight_grad(3, gw_send1, 2)
    gw_recv1[ix] = gw_send1[ix]
    exch_g1("start")
    forward(7)
    backward(7)
    weight_grad(1, gw_send2, 1)
    gu = atom_grad[:, 0:1] * ro_f[0:1, :]
    s = gate[...]
    gg_st[0] = (gu * s + gate_grad[...] * s * (1.0 - s)).astype(BF)
    weight_grad(0, gw_send2, 0)
    gw_recv2[ix] = gw_send2[ix]
    exch_g2("start")

    coefficients(7, [g_st[m] for m in range(*CHUNKS[7])])
    coef_rows = jnp.zeros((16, 256), F32)
    valid = jnp.where(iota((16, 256), 1) < 25, 1.0, 0.0)
    for j in range(8):
        part = jnp.concatenate([coef[pl.ds(j, 16, stride=8), :], jnp.zeros((16, 128), F32)], axis=1) * valid
        coef_rows = coef_rows + (part if j == 0 else pltpu.roll(part, 25 * j, 1))
    coef_pad = jnp.concatenate([coef_rows, jnp.zeros((112, 256), F32)], axis=0).astype(BF)
    answer = dot(own_hot[...], coef_pad).astype(BF)
    for k in range(ny):
        s_c[k] = answer[k * 16:(k + 1) * 16, :]
    r_c[iy] = s_c[iy]
    exch_c("start")

    def total_of(ref, n):
        total = ref[0].astype(F32)
        for k in range(1, n):
            total = total + ref[k].astype(F32)
        return total

    exch_g1("recv")
    sum_y1[iy] = total_of(gw_recv1, nx).astype(BF)
    exch_u1("start")
    exch_g2("recv")
    sum_y2[iy] = total_of(gw_recv2, nx).astype(BF)
    exch_u2("start")

    exch_c("recv")
    rows = dot(back, r_c[...].reshape(256, 256)).astype(BF)
    for k in range(nx):
        s_d[k] = rows[k * 32:(k + 1) * 32, :]
    r_d[ix] = s_d[ix]
    exch_d("start")

    for c in range(len(CHUNKS)):
        for copy in y_copies(c):
            copy.wait_send()
    exch_c("send")
    exch_g1("send")
    exch_g2("send")

    exch_u1("recv")
    out_recv1[ix] = total_of(sum_y1, ny).astype(BF)
    exch_o1("start")
    exch_u2("recv")
    out_recv2[ix] = total_of(sum_y2, ny).astype(BF)
    exch_o2("start")

    exch_d("recv")
    fetched = dot(pick_p[...], r_d[...].reshape(256, 256)).astype(BF)
    keep = jnp.where(iota((16, 256), 0) % 4 == iota((16, 256), 1) // 64, 1.0, 0.0)
    for q in range(8):
        rows16 = fetched[q * 16:(q + 1) * 16, 0:200]
        for r in range(4):
            t = q * 4 + r
            out = dot(rows16, basis[t])
            wanted = keep * jnp.where(iota((16, 256), 0) // 4 == r, 1.0, 0.0)
            dens[t:t + 1, :] = jnp.sum(out * wanted, axis=0, keepdims=True)
    folded = dens[:, 0:128] + dens[:, 128:256]
    tmp256[0:32, :] = folded + pltpu.roll(folded, 64, 1)
    even = tmp256[pl.ds(0, 16, stride=2), :]
    odd_rows = tmp256[pl.ds(1, 16, stride=2), :]
    dens_out[...] = jnp.where(iota((16, 128), 1) < 64, even, odd_rows)

    exch_d("send")
    exch_u1("send")
    exch_u2("send")
    exch_o1("recv")
    exch_o2("recv")
    exch_o1("send")
    exch_o2("send")


def spread_kernel(low, high, dens, dens_out, gw_out):
    dens_out[...] = dens[...]
    for ref, degrees in ((low, (0, 1)), (high, (2, 4, 3))):
        for at, l in enumerate(degrees):
            for k in range(ref.shape[0]):
                gw_out[l, k * 16:(k + 1) * 16, :] = ref[k, at * 16:(at + 1) * 16, :].astype(F32)


def body(nx, ny, irreps, mix_weight, readout, ghost_x, ghost_y, edge_source_row, edge_dst, radial,
         tile_peer, tile_block, tile_count, basis, density_cot):
    irr = jnp.transpose(irreps[0, 0], (1, 0, 2))
    nch = len(CHUNKS)
    dma = pltpu.SemaphoreType.DMA
    vm = pltpu.VMEM
    dens, low, high = pl.pallas_call(
        functools.partial(kernel, nx, ny),
        out_shape=(
            pltpu.VMEM((16, 128), F32),
            pltpu.VMEM((nx, 32, 128), BF),
            pltpu.VMEM((nx, 48, 128), BF),
        ),
        in_specs=[pl.BlockSpec(memory_space=pltpu.HBM)] * 13,
        out_specs=(pl.BlockSpec(memory_space=pltpu.VMEM),) * 3,
        scratch_shapes=[
            vm((5, 128, 128), BF),
            vm((25, 128), BF),
            vm((2, 64), jnp.int32), vm((2, 64), jnp.int32),
            vm((16, 128), jnp.int32), vm((16, 128), jnp.int32),
            vm((25, 1, 2048), F32),
            vm((4, 32), jnp.int32), vm((4, 32), jnp.int32), vm((1, 32), jnp.int32),
            vm((32, 200, 256), BF),
            vm((1, 2048), BF),
            vm((25, 384, 128), BF),
            vm((3200, 128), BF),
            vm((25, 128, 128), BF),
            vm((25, 128, 128), BF),
            vm((128, 128), BF),
            vm((128, 256), BF),
            vm((2048, 384), BF),
            vm((128, 2048), BF),
            vm((640, 2048), BF),
            vm((25, 128, 384), BF),
            vm((25, 128, 128), BF),
            vm((25, 128, 128), F32),
            vm((25, 128, 128), BF),
            vm((128, 128), F32),
            vm((128, 128), F32),
            vm((128, 128), F32),
            vm((128, 128), F32),
            vm((256, 128), F32),
            vm((nx, 32, 256), BF), vm((nx, 32, 256), BF),
            vm((ny, 16, 256), BF), vm((ny, 16, 256), BF),
            vm((ny, 16, 256), BF), vm((ny, 16, 256), BF),
            vm((nx, 32, 256), BF), vm((nx, 32, 256), BF),
            vm((128, 256), BF),
            vm((256, 128), BF),
            vm((32, 256), F32),
            vm((nx, 48, 128), BF), vm((nx, 48, 128), BF),
            vm((nx, 32, 128), BF), vm((nx, 32, 128), BF),
            vm((ny, 48, 128), BF), vm((ny, 32, 128), BF),
            dma((13,)),
            dma((nch, 2)), dma((nch, 2)), dma((nch, 2)), dma((nch, 2)),
            dma((1,)), dma((1,)), dma((1,)), dma((1,)), dma((1,)), dma((1,)), dma((1,)), dma((1,)),
            dma((2,)), dma((2,)), dma((2,)), dma((2,)), dma((2,)), dma((2,)),
        ],
        compiler_params=pltpu.CompilerParams(
            collective_id=0, has_side_effects=True, vmem_limit_bytes=60 * 1024 * 1024
        ),
    )(
        irr,
        mix_weight,
        readout,
        ghost_x.reshape(2, 64),
        ghost_y.reshape(2, 64),
        edge_source_row.reshape(16, 128),
        edge_dst.reshape(16, 128),
        radial.reshape(25, 1, 2048),
        jnp.transpose(tile_peer[0, 0]),
        jnp.transpose(tile_block[0, 0]),
        tile_count.reshape(1, 32),
        basis.reshape(32, 200, 256),
        density_cot.reshape(1, 2048),
    )
    dens, gw = pl.pallas_call(
        spread_kernel,
        out_shape=(
            jax.ShapeDtypeStruct((16, 128), F32),
            jax.ShapeDtypeStruct((5, 128, 128), F32),
        ),
        compiler_params=pltpu.CompilerParams(vmem_limit_bytes=4 * 1024 * 1024),
    )(low, high, dens)
    return dens.reshape(1, 1, 2048), gw


def solution(mesh):
    nx, ny = mesh.shape["gx"], mesh.shape["gy"]
    placed = (
        P("gx", "gy", None, None, None),
        P(),
        P(),
        P("gx", "gy", None, None),
        P("gx", "gy", None, None),
        P("gx", "gy", None),
        P("gx", "gy", None),
        P("gx", "gy", None, None),
        P("gx", "gy", None, None),
        P("gx", "gy", None, None),
        P("gx", "gy", None),
        P("gx", "gy", None, None, None),
        P("gx", "gy", None),
    )
    return jax.shard_map(
        functools.partial(body, nx, ny),
        mesh=mesh, in_specs=placed, out_specs=(P("gx", "gy", None), P()), check_vma=False,
    )
```
